32 devices in a mesh: side: 2 (over y), row: 4 (over z), col: 4 (over x, core).
Axes of the slice: x: 2, y: 2, z: 4, core: 2. Of those that a mesh axis runs over, the one named last changes fastest.
Arguments:
- queries: bfloat16 [64, 8192], P(('row', 'col')), may hold values from -4.5 to 16
- new_entries: bfloat16 [64, 2048], P(('row', 'col')), may hold values from -4.5 to 15.875
- cache_keys: bfloat16 [2, 64, 256, 1024], P('side', ('row', 'col')), may hold values from -4.5 to 16
- cache_values: bfloat16 [2, 64, 256, 1024], P('side', ('row', 'col')), may hold values from -6 to 6
- lengths: int32 [64], P(('row', 'col')), may hold values from 1 to 256, 4096 in all
- residual: bfloat16 [64, 8192], P(None, 'col'), may hold values from -16 to 16
- norm_gain: bfloat16 [8192], P('col'), may hold values from 0.099609375 to 1.8984375
- out_weight: bfloat16 [2, 8192, 8192], P('side', 'row', 'col'), may hold values from -0.125 to 0.125
- gate_weight: bfloat16 [2, 8192, 14336], P('side', 'col', 'row'), may hold values from -0.0625 to 0.0625
- up_weight: bfloat16 [2, 8192, 14336], P('side', 'col', 'row'), may hold values from -0.0625 to 0.0625
- down_weight: bfloat16 [2, 14336, 8192], P('side', 'row', 'col'), may hold values from -0.046875 to 0.046875
Outputs:
- layer_out: bfloat16 [64, 8192], P(('row', 'col'), 'side')
The draws below stay inside these ranges and needn't reach their ends.
All inputs are finite; a program needn't handle non-finite values. No bound on the sum of `lengths` on one device may be relied on, other than what follows from the above.
Results may differ from the reference program's by a relative error of at most 0.025.
Values may be sent and summed in bfloat16 or wider, within the bound.
A program may use at most 128 MiB of HBM per device.

```python
import math
import jax
import jax.numpy as jnp
import numpy as np
from jax import lax

D = 8192
H = 64
KVH = 8
HD = 128
FF = 14336
CAP = 256
REQ_DEV = 4
REQS = 64
ORIG = 64
N_ROW = 4
N_COL = 4


def draw_queries(key, part):
    inner_key = jax.random.fold_in(key, 1)
    base = jnp.clip(jax.random.normal(inner_key, (REQS, H, HD), jnp.float32), -4.5, 4.5)
    return base.reshape(REQS, H * HD).astype(jnp.bfloat16)


def draw_new_entries(key, part):
    inner_key = jax.random.fold_in(key, 2)
    base = jnp.clip(jax.random.normal(inner_key, (REQS, 2, KVH, HD), jnp.float32), -4.5, 4.5)
    return base.reshape(REQS, 2 * KVH * HD).astype(jnp.bfloat16)


def draw_cache_keys(key, part):
    inner_key = jax.random.fold_in(key, 3)
    base = jnp.clip(jax.random.normal(inner_key, (2, REQS, CAP, KVH, HD), jnp.float32), -4.5, 4.5)
    return base.reshape(2, REQS, CAP, KVH * HD).astype(jnp.bfloat16)


def draw_residual(key, part):
    column = jnp.arange(D).astype(jnp.float32) / (D - 1)
    rise = jax.random.uniform(jax.random.fold_in(key, 41), (REQS, 1), jnp.float32, 0.0, 1.0)
    row_scale = 0.2 * 10.0 ** rise
    noise = jnp.clip(jax.random.normal(jax.random.fold_in(key, 4), (REQS, D), jnp.float32), -3.0, 3.0)
    col_scale = 0.2 * 10.0 ** column
    values = noise * row_scale * col_scale[None, :]
    return jnp.clip(values, -16.0, 16.0).astype(jnp.bfloat16)


def steps_of(stream_key, shape, cuts, least, high):
    level, own = 1.0, jax.random.fold_in(stream_key, 6)
    for axis_at, shards_of in cuts:
        steps = jnp.exp(jax.random.uniform(jax.random.fold_in(own, axis_at), (shards_of,), jnp.float32, least / len(cuts), high / len(cuts)))
        level = level * jnp.repeat(steps, shape[axis_at] // shards_of).reshape([-1 if axis == axis_at else 1 for axis in range(len(shape))])
    return level


def profile(number_of, total, reach, lean):
    loads = [(1 << 20) // math.isqrt(standing ** lean) + 1 for standing in range(2, number_of + 1)]
    spare, counts = total - reach - (number_of - 1), [1] * (number_of - 1)
    while spare > 0:
        free = [i for i in range(number_of - 1) if counts[i] < reach]
        whole, remaining = sum([loads[i] for i in free]), spare
        for i in free:
            more = min(reach - counts[i], max(1, remaining * loads[i] // whole), spare)
            counts[i] = counts[i] + more
            spare = spare - more
    return np.array([reach] + counts)


def uneven(stream_key, number_of, total, most, slope):
    if number_of == 2:
        one = jax.random.randint(stream_key, (), max(1, total - most), min(most, total - 1) + 1)
        return jnp.stack([one, total - one])
    sizes = jnp.asarray(profile(number_of, total, most, slope), jnp.int32)
    twos = (number_of - 1) // 2
    giver, taker = sizes[1:1 + 2 * twos:2], sizes[2:2 + 2 * twos:2]
    margin = jnp.minimum(giver - 1, most - taker)
    passed = jax.random.randint(jax.random.fold_in(stream_key, 1), (twos,), 0, 1 << 20) % (margin + 1)
    sizes = sizes.at[1:1 + 2 * twos:2].set(giver - passed).at[2:2 + 2 * twos:2].set(taker + passed)
    return sizes[jax.random.permutation(jax.random.fold_in(stream_key, 2), number_of)]


def centred(own_key, shape, scale, most, split=(), kind=jnp.bfloat16):
    factor_of = steps_of(own_key, shape, split, -0.22, 0.18) if split else 1.0
    values = jax.random.normal(own_key, shape, jnp.float32) * scale * factor_of
    return jnp.minimum(jnp.maximum(values, -most), most).astype(kind)


def setup_inputs(seed: int = 0) -> dict:
    seeds = jax.random.split(jax.random.key(seed), 12)
    queries = draw_queries(jax.random.fold_in(seeds[11], 71), 0)
    new_entries = draw_new_entries(jax.random.fold_in(seeds[11], 71), 0)
    cache_keys = draw_cache_keys(jax.random.fold_in(seeds[11], 71), 0)
    cache_values = centred(seeds[3], (2, REQS, CAP, KVH * HD), 1.0, 6.0, ((0, 2), (1, 16)))
    lengths = uneven(seeds[4], REQS, REQS * CAP // 4, CAP, 2).astype(jnp.int32)
    residual = draw_residual(jax.random.fold_in(seeds[11], 71), 0)
    norm_gain = jnp.clip(1.0 + 0.18 * jax.random.normal(seeds[6], (D,), jnp.float32), 0.099609375, 1.8984375).astype(jnp.bfloat16)
    out_weight = centred(seeds[7], (2, H * HD, D), (H * HD // 4) ** -0.5, 0.125, ((0, 2), (1, 4), (2, 4)))
    gate_weight = centred(seeds[8], (2, D, FF), D ** -0.5, 0.0625, ((0, 2), (1, 4), (2, 4)))
    up_weight = centred(seeds[9], (2, D, FF), D ** -0.5, 0.0625, ((0, 2), (1, 4), (2, 4)))
    down_weight = centred(seeds[10], (2, FF, D), FF ** -0.5, 0.046875, ((0, 2), (1, 4), (2, 4)))
    return dict(queries=queries, new_entries=new_entries, cache_keys=cache_keys, cache_values=cache_values, lengths=lengths, residual=residual, norm_gain=norm_gain, out_weight=out_weight, gate_weight=gate_weight, up_weight=up_weight, down_weight=down_weight)


rope_theta = 500000.0
stretch_factor = 8.0
eps = 1e-05

def frequencies(lengths):
    seq = lengths.astype(jnp.float32) + 1.0
    stretch = jnp.maximum(stretch_factor * seq / ORIG - (stretch_factor - 1.0), 1.0)
    log_base = jnp.log(jnp.float32(rope_theta)) + HD / (HD - 2.0) * jnp.log(stretch)
    expo = jnp.arange(HD // 2).astype(jnp.float32) * (2.0 / HD)
    return jnp.exp(-expo[None, :] * log_base[:, None])

def rotary(vec, angles):
    half = vec.shape[-1] // 2
    first = vec[..., :half]
    second = vec[..., half:]
    cosine = jnp.cos(angles)
    sine = jnp.sin(angles)
    return jnp.concatenate([first * cosine - second * sine, second * cosine + first * sine], axis=-1)

def attention(queries, new_entries, keys, values, lengths):
    slots = queries.shape[0]
    span = keys.shape[1]
    per_group = H // KVH
    freqs = frequencies(lengths)
    angle_new = lengths.astype(jnp.float32)[:, None] * freqs
    angle_cache = jnp.arange(span).astype(jnp.float32)[None, :, None] * freqs[:, None, :]
    query_rot = rotary(queries.astype(jnp.float32).reshape(slots, H, HD), angle_new[:, None, :])
    query_rot = lax.optimization_barrier(query_rot.astype(jnp.bfloat16)).astype(jnp.float32)
    query_rot = query_rot.reshape(slots, KVH, per_group, HD)
    key_fresh = new_entries[:, :KVH * HD].astype(jnp.float32).reshape(slots, KVH, HD)
    value_fresh = new_entries[:, KVH * HD:].astype(jnp.float32).reshape(slots, KVH, HD)
    key_new_rot = rotary(key_fresh, angle_new[:, None, :])
    key_new_rot = lax.optimization_barrier(key_new_rot.astype(jnp.bfloat16)).astype(jnp.float32)
    key_rot = rotary(keys.astype(jnp.float32).reshape(slots, span, KVH, HD), angle_cache[:, :, None, :])
    key_rot = lax.optimization_barrier(key_rot.astype(jnp.bfloat16)).astype(jnp.float32)
    scale = HD ** (-0.5)
    scores = jnp.einsum('sgqd,scgd->sgqc', query_rot, key_rot) * scale
    own_score = jnp.einsum('sgqd,sgd->sgq', query_rot, key_new_rot) * scale
    valid_mask = (jnp.arange(span)[None, :] < lengths[:, None])[:, None, None, :]
    highest = jnp.maximum(lax.optimization_barrier(jnp.max(jnp.where(valid_mask, scores, -1e+30), axis=-1)), own_score)
    weights = jnp.where(valid_mask, jnp.exp(scores - highest[..., None]), 0.0)
    own_weight = jnp.exp(own_score - highest)
    totals = lax.optimization_barrier(jnp.sum(weights, axis=-1)) + own_weight
    weights16 = lax.optimization_barrier(weights.astype(jnp.bfloat16)).astype(jnp.float32)
    cached_values = values.astype(jnp.float32).reshape(slots, span, KVH, HD)
    mixed = jnp.einsum('sgqc,scgd->sgqd', weights16, cached_values)
    mixed = mixed + own_weight[..., None] * value_fresh[:, :, None, :]
    return (mixed / totals[..., None]).reshape(slots, H * HD).astype(jnp.bfloat16)

def rounded(value):
    return lax.optimization_barrier(value.astype(jnp.bfloat16)).astype(jnp.float32)

def reference(queries, new_entries, cache_keys, cache_values, lengths, residual, norm_gain, out_weight, gate_weight, up_weight, down_weight):
    groups = REQS // REQ_DEV

    def one_block(pieces):
        return attention(pieces[0], pieces[1], pieces[2], pieces[3], pieces[4])
    attended = lax.map(one_block, (queries.reshape(groups, REQ_DEV, H * HD), new_entries.reshape(groups, REQ_DEV, 2 * KVH * HD), cache_keys[0].reshape(groups, REQ_DEV, CAP, KVH * HD), cache_values[0].reshape(groups, REQ_DEV, CAP, KVH * HD), lengths.reshape(groups, REQ_DEV)))
    attended = attended.reshape(REQS, H * HD)
    head_block = H * HD // N_ROW
    projected = jnp.zeros((REQS, D), jnp.float32)
    for block in range(N_ROW):
        lower = block * head_block
        term = jnp.dot(attended[:, lower:lower + head_block], out_weight[1, lower:lower + head_block, :], preferred_element_type=jnp.float32)
        projected = projected + rounded(term)
    stream = residual.astype(jnp.float32) + projected
    inv_rms = lax.rsqrt(lax.optimization_barrier(jnp.sum(stream * stream, axis=1)) / D + eps)
    normed = (stream * inv_rms[:, None] * norm_gain.astype(jnp.float32)[None, :]).astype(jnp.bfloat16)
    col_block = D // N_COL
    gate_sum = jnp.zeros((REQS, FF), jnp.float32)
    up_sum = jnp.zeros((REQS, FF), jnp.float32)
    for block in range(N_COL):
        lower = block * col_block
        rows_in = normed[:, lower:lower + col_block]
        gate_sum = gate_sum + rounded(jnp.dot(rows_in, gate_weight[1, lower:lower + col_block, :], preferred_element_type=jnp.float32))
        up_sum = up_sum + rounded(jnp.dot(rows_in, up_weight[1, lower:lower + col_block, :], preferred_element_type=jnp.float32))
    hidden = (jax.nn.silu(gate_sum) * up_sum).astype(jnp.bfloat16)
    unit_block = FF // N_ROW
    down_sum = jnp.zeros((REQS, D), jnp.float32)
    for block in range(N_ROW):
        lower = block * unit_block
        term = jnp.dot(hidden[:, lower:lower + unit_block], down_weight[1, lower:lower + unit_block, :], preferred_element_type=jnp.float32)
        down_sum = down_sum + rounded(term)
    return (stream + down_sum).astype(jnp.bfloat16)
```

```python
import jax
import jax.numpy as jnp
from jax import lax
from jax.experimental import pallas as pl
from jax.experimental.pallas import tpu as pltpu
from jax.sharding import PartitionSpec as P

D = 8192
H = 64
KVH = 8
HD = 128
ORIG = 64


rope_theta = 500000.0
stretch_factor = 8.0
eps = 1e-05


def frequencies(lengths):
    seq = lengths.astype(jnp.float32) + 1.0
    stretch = jnp.maximum(stretch_factor * seq / ORIG - (stretch_factor - 1.0), 1.0)
    log_base = jnp.log(jnp.float32(rope_theta)) + HD / (HD - 2.0) * jnp.log(stretch)
    expo = jnp.arange(HD // 2).astype(jnp.float32) * (2.0 / HD)
    return jnp.exp(-expo[None, :] * log_base[:, None])


def rotary(vec, angles):
    half = vec.shape[-1] // 2
    first = vec[..., :half]
    second = vec[..., half:]
    cosine = jnp.cos(angles)
    sine = jnp.sin(angles)
    return jnp.concatenate(
        [first * cosine - second * sine, second * cosine + first * sine], axis=-1
    )


def attention(queries, new_entries, keys, values, lengths):
    slots = queries.shape[0]
    span = keys.shape[1]
    per_group = H // KVH
    freqs = frequencies(lengths)
    angle_new = lengths.astype(jnp.float32)[:, None] * freqs
    angle_cache = jnp.arange(span).astype(jnp.float32)[None, :, None] * freqs[:, None, :]
    query_rot = rotary(
        queries.astype(jnp.float32).reshape(slots, H, HD), angle_new[:, None, :]
    ).astype(jnp.bfloat16)
    query_rot = query_rot.reshape(slots, KVH, per_group, HD)
    key_fresh = new_entries[:, : KVH * HD].astype(jnp.float32).reshape(slots, KVH, HD)
    value_fresh = new_entries[:, KVH * HD :].astype(jnp.float32).reshape(slots, KVH, HD)
    key_new_rot = rotary(key_fresh, angle_new[:, None, :]).astype(jnp.bfloat16)
    key_rot = rotary(
        keys.astype(jnp.float32).reshape(slots, span, KVH, HD), angle_cache[:, :, None, :]
    ).astype(jnp.bfloat16)
    scale = HD ** (-0.5)
    scores = (
        jnp.einsum("sgqd,scgd->sgqc", query_rot, key_rot, preferred_element_type=jnp.float32)
        * scale
    )
    own_score = (
        jnp.einsum("sgqd,sgd->sgq", query_rot, key_new_rot, preferred_element_type=jnp.float32)
        * scale
    )
    valid_mask = (jnp.arange(span)[None, :] < lengths[:, None])[:, None, None, :]
    highest = jnp.maximum(jnp.max(jnp.where(valid_mask, scores, -1e30), axis=-1), own_score)
    weights = jnp.where(valid_mask, jnp.exp(scores - highest[..., None]), 0.0)
    own_weight = jnp.exp(own_score - highest)
    totals = jnp.sum(weights, axis=-1) + own_weight
    weights16 = weights.astype(jnp.bfloat16)
    mixed = jnp.einsum(
        "sgqc,scgd->sgqd",
        weights16,
        values.reshape(slots, span, KVH, HD),
        preferred_element_type=jnp.float32,
    )
    mixed = mixed + own_weight[..., None] * value_fresh[:, :, None, :]
    return (mixed / totals[..., None]).reshape(slots, H * HD).astype(jnp.bfloat16)


MESH = pl.DeviceIdType.MESH
F32 = jnp.float32
BF16 = jnp.bfloat16


def tile_of(width):
    return next(t for t in (512, 256, 128) if width % t == 0)


def layer_kernel(
    rows, cols, att, residual, gain, out_hbm, gate_hbm, up_hbm, down_hbm, out,
    w_out, w_gate, w_up, w_down,
    xg, xf, xb, part, rs_in, stream, sq_out, sq_in, inv_all, xs,
    gu, core_in, sum_out, x_in, hid, acc, dn, dn_in, fin, fin_in,
    w_sem, s1, r1, s2, r2, s3, r3, s4, r4, s5, r5, s6, r6, s7, r7,
    sa, ra, sb, rb, sc, rc_, sd, rd, s8, r8, s9, r9,
):
    side, row, col = (lax.axis_index(n) for n in ("side", "row", "col"))
    his = cols // 2
    core, hi = col % 2, col // 2
    mate = hi * 2 + (1 - core)
    half = cols // 2

    def at(s, r, c):
        return {"side": s, "row": r, "col": c}

    def rcopy(src, dst, ss, rs, dev):
        return pltpu.make_async_remote_copy(
            src_ref=src, dst_ref=dst, send_sem=ss, recv_sem=rs, device_id=dev, device_id_type=MESH
        )

    def row_peer(d):
        return lax.rem(row + d, rows)

    def col_peer(d):
        return lax.rem(col + d, cols)

    def hi_peer(d):
        return lax.rem(hi + d, his) * 2 + core

    weights = [
        pltpu.make_async_copy(h.at[0], w, w_sem.at[i])
        for i, (h, w) in enumerate(
            ((out_hbm, w_out), (gate_hbm, w_gate), (up_hbm, w_up), (down_hbm, w_down))
        )
    ]

    @pl.when(side == 1)
    def _():
        for copy in weights:
            copy.start()

    barrier = pltpu.get_barrier_semaphore()

    def greet(dev):
        pl.semaphore_signal(barrier, inc=1, device_id=dev, device_id_type=MESH)

    for d in range(rows):
        greet(at(1 - side, row_peer(d), col))
    for d in range(1, cols):
        greet(at(1 - side, row, col_peer(d)))

    @pl.when(side == 1)
    def _():
        for d in range(1, rows):
            greet(at(1, row_peer(d), col))
        for d in range(1, cols):
            greet(at(1, row, col_peer(d)))
        pl.semaphore_wait(barrier, 2 * (rows + cols) - 3)

    @pl.when(side == 0)
    def _():
        pl.semaphore_wait(barrier, rows + cols - 1)

    group = residual.shape[0] // rows
    slots = group // cols
    quarter = residual.shape[0] // cols
    width = residual.shape[1]
    heads = att.shape[2]

    def head_copy(d):
        return rcopy(att.at[row_peer(d)], xg.at[row, col], s1.at[d], r1.at[d], at(1, row_peer(d), col))

    @pl.when(side == 0)
    def _():
        for d in range(rows):
            head_copy(d).start()
        for d in range(rows):
            head_copy(d).wait_send()

    @pl.when(side == 1)
    def _():
        for d in range(rows):
            head_copy(d).wait_recv()
        mine = xg.at[:, col]
        own = rcopy(mine, mine, s2.at[0], r2.at[0], at(1, row, mate))
        own.start()
        across = [
            rcopy(mine, mine, s2.at[d], r2.at[d], at(1, row, hi_peer(d))) for d in range(1, his)
        ]
        for copy in across:
            copy.start()
        passed = []
        for d in range(1, his):
            across[d - 1].wait_recv()
            got = xg.at[:, hi_peer(his - d)]
            copy = rcopy(got, got, s2.at[his + d - 1], r2.at[his + d - 1], at(1, row, mate))
            copy.start()
            passed.append(copy)
        own.wait_recv()
        for copy in passed:
            copy.wait_recv()
        total = rows * cols * slots
        xf[...] = xg[...].astype(F32).reshape(total * heads, HD)
        for h in range(heads):
            xb[:, h * HD : (h + 1) * HD] = xf[pl.ds(h, total, stride=heads), :].astype(BF16)

        tiles, tile = part.shape[0], part.shape[3]
        weights[0].wait()

        def proj_copy(j, d):
            return rcopy(
                part.at[j, row_peer(d)], rs_in.at[d - 1, j], s3.at[d - 1, j], r3.at[d - 1, j],
                at(1, row_peer(d), col),
            )

        @pl.loop(0, tiles)
        def _(j):
            w = w_out[:, pl.ds(pl.multiple_of(j * tile, tile), tile)]
            res = jnp.dot(xb[...], w, preferred_element_type=F32).astype(BF16)
            part[j] = res.reshape(rows, group, tile)
            for d in range(1, rows):
                proj_copy(j, d).start()

        squares = jnp.zeros((group, 1), F32)
        my_rows = pl.ds(pl.multiple_of(row * group, group), group)
        for j in range(tiles):
            value = part[j, row].astype(F32)
            for d in range(1, rows):
                proj_copy(j, d).wait_recv()
                value = value + rs_in[d - 1, j].astype(F32)
            lanes = slice(j * tile, (j + 1) * tile)
            value = value + residual[my_rows, lanes].astype(F32)
            stream[:, lanes] = value
            squares = squares + jnp.sum(value * value, axis=1, keepdims=True)
            xs[row, :, lanes] = (value * gain[:, lanes].astype(F32)).astype(BF16)
        sq_out[...] = jnp.broadcast_to(squares, sq_out.shape)

        def stream_copy(d):
            return rcopy(
                xs.at[row], xs.at[row], s4.at[d - 1], r4.at[d - 1], at(1, row_peer(d), col)
            )

        def square_copy(d):
            return rcopy(
                sq_out, sq_in.at[d - 1], s5.at[d - 1], r5.at[d - 1], at(1, row, col_peer(d))
            )

        def inv_copy(d):
            return rcopy(
                inv_all.at[row], inv_all.at[row], s6.at[d - 1], r6.at[d - 1],
                at(1, row_peer(d), col),
            )

        for d in range(1, cols):
            square_copy(d).start()
        for d in range(1, rows):
            stream_copy(d).start()
        sums = sq_out[...]
        for d in range(1, cols):
            square_copy(d).wait_recv()
            sums = sums + sq_in[d - 1]
        inv_all[row] = lax.rsqrt(sums / D + eps)
        for d in range(1, rows):
            inv_copy(d).start()
        for d in range(1, rows):
            stream_copy(d).wait_recv()
        for d in range(1, rows):
            inv_copy(d).wait_recv()
        weights[1].wait()
        weights[2].wait()
        weights[3].wait()

        steps, unit = gu.shape[0], gu.shape[5]

        def core_copy(j):
            return rcopy(gu.at[j, 1 - core], core_in.at[j], sa.at[j], ra.at[j], at(1, row, mate))

        def x_copy(j, d):
            there = lax.rem(hi + d, his)
            return rcopy(
                sum_out.at[j, there], x_in.at[d - 1, j], sb.at[d - 1, j], rb.at[d - 1, j],
                at(1, row, hi_peer(d)),
            )

        def hid_copy(j, d):
            dev = mate if d == 0 else hi_peer(d)
            return rcopy(hid.at[j, col], hid.at[j, col], sc.at[d, j], rc_.at[d, j], at(1, row, dev))

        def fwd_copy(j, d):
            got = hid.at[j, hi_peer(his - d)]
            return rcopy(got, got, sd.at[d - 1, j], rd.at[d - 1, j], at(1, row, mate))

        acc[...] = jnp.zeros_like(acc)
        lags = (0, 1, 3, 5, 6)

        @pl.loop(0, steps + lags[4])
        def _(i):
            def stage(k):
                j = i - lags[k]
                return j, jnp.logical_and(j >= 0, j < steps)

            j0, on0 = stage(0)

            @pl.when(on0)
            def _():
                at_cols = pl.ds(pl.multiple_of(j0 * unit, unit), unit)
                x = xs[...].reshape(rows * group, width)
                scale = inv_all[...].reshape(rows * group, HD)[:, :1]
                for n, w in enumerate((w_gate, w_up)):
                    res = jnp.dot(x, w[:, at_cols], preferred_element_type=F32) * scale
                    res = res.astype(BF16)
                    for q in range(cols):
                        gu[j0, q % 2, q // 2, n] = res[q * quarter : (q + 1) * quarter]
                core_copy(j0).start()

            j1, on1 = stage(1)

            @pl.when(on1)
            def _():
                core_copy(j1).wait_recv()
                sum_out[j1] = (gu[j1, core].astype(F32) + core_in[j1].astype(F32)).astype(BF16)
                for d in range(1, his):
                    x_copy(j1, d).start()

            j2, on2 = stage(2)

            @pl.when(on2)
            def _():
                both = sum_out[j2, hi].astype(F32)
                for d in range(1, his):
                    x_copy(j2, d).wait_recv()
                    both = both + x_in[d - 1, j2].astype(F32)
                gate, up = both[0], both[1]
                hid[j2, col] = (gate / (1.0 + jnp.exp(-gate)) * up).astype(BF16)
                for d in range(his):
                    hid_copy(j2, d).start()

            j3, on3 = stage(3)

            @pl.when(on3)
            def _():
                for d in range(1, his):
                    hid_copy(j3, d).wait_recv()
                    fwd_copy(j3, d).start()

            j4, on4 = stage(4)

            @pl.when(on4)
            def _():
                hid_copy(j4, 0).wait_recv()
                for d in range(1, his):
                    fwd_copy(j4, d).wait_recv()
                h = hid[j4].reshape(rows * group, unit)
                w = w_down[pl.ds(pl.multiple_of(j4 * unit, unit), unit), :]
                acc[...] += jnp.dot(h, w, preferred_element_type=F32)

        dn[...] = acc[...].astype(BF16).reshape(rows, group, width)

        def down_copy(d):
            return rcopy(
                dn.at[row_peer(d)], dn_in.at[d - 1], s7.at[d - 1], r7.at[d - 1],
                at(1, row_peer(d), col),
            )

        for d in range(1, rows):
            down_copy(d).start()
        last = stream[...] + dn[row].astype(F32)
        for d in range(1, rows):
            down_copy(d).wait_recv()
            last = last + dn_in[d - 1].astype(F32)
        last = last.astype(BF16).astype(F32)
        for c in range(cols):
            fin[c] = last[c * slots : (c + 1) * slots].astype(BF16)

        own.wait_send()
        for copy in across + passed:
            copy.wait_send()
        for d in range(1, rows):
            @pl.loop(0, tiles)
            def _(j):
                proj_copy(j, d).wait_send()
            stream_copy(d).wait_send()
            inv_copy(d).wait_send()
            down_copy(d).wait_send()
        for d in range(1, cols):
            square_copy(d).wait_send()

        @pl.loop(0, steps)
        def _(j):
            core_copy(j).wait_send()
            for d in range(his):
                hid_copy(j, d).wait_send()
            for d in range(1, his):
                x_copy(j, d).wait_send()
                fwd_copy(j, d).wait_send()

    def up_copy(d):
        return rcopy(
            fin.at[col_peer(d)], fin_in.at[col - half], s8.at[d - 1], r8.at[col - half],
            at(1, row, col_peer(d)),
        )

    def low_copy(d):
        return rcopy(
            fin.at[col_peer(d)], fin_in.at[col], s9.at[d], r8.at[col], at(0, row, col_peer(d))
        )

    @pl.when(side == 1)
    def _():
        @pl.when(col >= half)
        def _():
            for d in range(1, cols):
                up_copy(d).start()
            fin_in[col - half] = fin[col]
            for d in range(1, cols):
                up_copy(d).wait_send()

        @pl.when(col < half)
        def _():
            for d in range(cols):
                low_copy(d).start()
            for d in range(cols):
                low_copy(d).wait_send()

    for k in range(half):
        @pl.when(jnp.logical_or(side == 0, col != half + k))
        def _():
            rcopy(
                fin.at[0], fin_in.at[k], s9.at[0], r8.at[k], at(1 - side, row, col)
            ).wait_recv()
        out[:, k * width : (k + 1) * width] = fin_in[k]


def layer(rows, cols, att, residual, gain, out_w, gate_w, up_w, down_w):
    _, slots, heads, _ = att.shape
    total, width = residual.shape
    group, quarter, his = total // rows, total // cols, cols // 2
    ff = gate_w.shape[2]
    tile, unit = tile_of(width), tile_of(ff)
    tiles, steps = width // tile, ff // unit
    dma = pltpu.SemaphoreType.DMA
    vmem = pltpu.VMEM
    scratch = [
        vmem(out_w.shape[1:], BF16),
        vmem(gate_w.shape[1:], BF16),
        vmem(up_w.shape[1:], BF16),
        vmem(down_w.shape[1:], BF16),
        vmem((rows, cols, slots, heads, HD), BF16),
        vmem((total * heads, HD), F32),
        vmem((total, heads * HD), BF16),
        vmem((tiles, rows, group, tile), BF16),
        vmem((rows - 1, tiles, group, tile), BF16),
        vmem((group, width), F32),
        vmem((group, HD), F32),
        vmem((cols - 1, group, HD), F32),
        vmem((rows, group, HD), F32),
        vmem((rows, group, width), BF16),
        vmem((steps, 2, his, 2, quarter, unit), BF16),
        vmem((steps, his, 2, quarter, unit), BF16),
        vmem((steps, his, 2, quarter, unit), BF16),
        vmem((his - 1, steps, 2, quarter, unit), BF16),
        vmem((steps, cols, quarter, unit), BF16),
        vmem((total, width), F32),
        vmem((rows, group, width), BF16),
        vmem((rows - 1, group, width), BF16),
        vmem((cols, slots, width), BF16),
        vmem((cols // 2, slots, width), BF16),
        dma((4,)),
        dma((rows,)), dma((rows,)),
        dma((2 * his - 1,)), dma((2 * his - 1,)),
        dma((rows - 1, tiles)), dma((rows - 1, tiles)),
        dma((rows - 1,)), dma((rows - 1,)),
        dma((cols - 1,)), dma((cols - 1,)),
        dma((rows - 1,)), dma((rows - 1,)),
        dma((rows - 1,)), dma((rows - 1,)),
        dma((steps,)), dma((steps,)),
        dma((his - 1, steps)), dma((his - 1, steps)),
        dma((his, steps)), dma((his, steps)),
        dma((his - 1, steps)), dma((his - 1, steps)),
        dma((cols,)), dma((cols // 2,)),
        dma((cols,)), dma((1,)),
    ]
    in_vmem = pl.BlockSpec(memory_space=pltpu.VMEM)
    anywhere = pl.BlockSpec(memory_space=pl.ANY)

    def kernel(*refs):
        layer_kernel(rows, cols, *refs)

    weight_bytes = 2 * (out_w.size + gate_w.size + up_w.size + down_w.size)
    return pl.pallas_call(
        kernel,
        out_shape=jax.ShapeDtypeStruct((slots, width * cols // 2), BF16),
        in_specs=[in_vmem] * 3 + [anywhere] * 4,
        out_specs=in_vmem,
        scratch_shapes=scratch,
        compiler_params=pltpu.CompilerParams(
            collective_id=0, has_side_effects=True, vmem_limit_bytes=62 * 1024 * 1024
        ),
        cost_estimate=pl.CostEstimate(
            flops=total * weight_bytes, bytes_accessed=weight_bytes, transcendentals=0
        ),
        name="layer",
    )(att, residual, gain, out_w, gate_w, up_w, down_w)


def local(
    queries,
    new_entries,
    cache_keys,
    cache_values,
    lengths,
    residual,
    norm_gain,
    out_weight,
    gate_weight,
    up_weight,
    down_weight,
):
    attended = attention(queries, new_entries, cache_keys[0], cache_values[0], lengths)
    slots = attended.shape[0]
    rows = lax.axis_size("row")
    cols = lax.axis_size("col")
    att = attended.reshape(slots, rows, H // rows, HD).transpose(1, 0, 2, 3)
    return layer(
        rows, cols, att, residual, norm_gain[None, :],
        out_weight, gate_weight, up_weight, down_weight,
    )


def solution(mesh):
    in_specs = (
        P(("row", "col"), None),
        P(("row", "col"), None),
        P("side", ("row", "col"), None, None),
        P("side", ("row", "col"), None, None),
        P(("row", "col")),
        P(None, "col"),
        P("col"),
        P("side", "row", "col"),
        P("side", "col", "row"),
        P("side", "col", "row"),
        P("side", "row", "col"),
    )
    out_specs = P(("row", "col"), "side")
    return jax.shard_map(local, mesh=mesh, in_specs=in_specs, out_specs=out_specs, check_vma=False)
```

```python
import jax
import jax.numpy as jnp
from jax import lax
from jax.experimental import pallas as pl
from jax.experimental.pallas import tpu as pltpu
from jax.sharding import PartitionSpec as P

D = 8192
H = 64
KVH = 8
HD = 128
ORIG = 64


rope_theta = 500000.0
stretch_factor = 8.0
eps = 1e-05


MESH = pl.DeviceIdType.MESH
F32 = jnp.float32
BF16 = jnp.bfloat16


def tile_of(width):
    return next(t for t in (512, 256, 128) if width % t == 0)


def attention(
    rows, queries, entries, lengths, keys, values, qf, ef, att, key_hbm, value_hbm, c_sem, head_copy
):
    slots, span, _ = keys.shape
    per_group = H // KVH
    heads = H // rows
    for s in range(slots):
        for h in range(H):
            qf[s, h : h + 1, :] = queries[s : s + 1, h * HD : (h + 1) * HD].astype(F32)
        for h in range(2 * KVH):
            ef[s, h : h + 1, :] = entries[s : s + 1, h * HD : (h + 1) * HD].astype(F32)
    lane = lax.broadcasted_iota(jnp.int32, (1, HD), 1)
    lower = lane < HD // 2
    expo = jnp.where(lower, lane, lane - HD // 2).astype(F32) * (2.0 / HD)
    fine = 16
    step = lax.broadcasted_iota(jnp.int32, (fine, HD), 0).astype(F32)
    place = lax.broadcasted_iota(jnp.int32, (H, span), 1)
    scale = HD ** (-0.5)

    def rot(vec, cosine, sine):
        return vec * cosine + pltpu.roll(vec, HD // 2, 1) * sine

    def rounded(vec):
        return vec.astype(BF16).astype(F32)

    @pl.loop(0, slots)
    def _(s):
        length = jnp.full((1, HD), lengths[s], jnp.int32).astype(F32)
        stretch = jnp.maximum(stretch_factor * (length + 1.0) / ORIG - (stretch_factor - 1.0), 1.0)
        log_base = jnp.log(jnp.full((1, HD), rope_theta, F32)) + HD / (HD - 2.0) * jnp.log(stretch)
        freq = jnp.exp(-expo * log_base)
        cos_new = jnp.cos(length * freq)
        sin_new = jnp.sin(length * freq)
        sin_new = jnp.where(lower, -sin_new, sin_new)
        cos_b, sin_b = jnp.cos(step * freq), jnp.sin(step * freq)
        cos_a, sin_a = jnp.cos(step * (fine * freq)), jnp.sin(step * (fine * freq))
        sign = jnp.where(lower, -1.0, 1.0)
        sin_b_signed, cos_b_signed = sin_b * sign, cos_b * sign
        cos_t, sin_t = [], []
        for a in range(span // fine):
            ca, sa = cos_a[a : a + 1], sin_a[a : a + 1]
            cos_t.append(ca * cos_b - sa * sin_b)
            sin_t.append(sa * cos_b_signed + ca * sin_b_signed)
        cos_t = jnp.concatenate(cos_t, axis=0)
        sin_t = jnp.concatenate(sin_t, axis=0)

        q = rounded(rot(qf[s], cos_new, sin_new))
        new = ef[s]
        key_new = rounded(rot(new[:KVH], cos_new, sin_new))
        value_new = new[KVH:]
        pltpu.make_async_copy(key_hbm.at[0, s], keys.at[s], c_sem.at[0, s]).wait()
        scores, own = [], []
        for g in range(KVH):
            q_g = q[g * per_group : (g + 1) * per_group]
            key = keys[s, :, g * HD : (g + 1) * HD].astype(F32)
            key = rot(key, cos_t, sin_t).astype(BF16)
            scores.append(
                lax.dot_general(
                    q_g.astype(BF16), key, (((1,), (1,)), ((), ())), preferred_element_type=F32
                )
            )
            own.append(jnp.sum(q_g * key_new[g : g + 1], axis=1, keepdims=True))
        scores = jnp.concatenate(scores, axis=0) * scale
        own = jnp.concatenate(own, axis=0) * scale
        valid = place < jnp.full((H, span), lengths[s], jnp.int32)
        top = jnp.maximum(jnp.max(jnp.where(valid, scores, -1e30), axis=1, keepdims=True), own)
        weight = jnp.where(valid, jnp.exp(scores - top), 0.0)
        own_weight = jnp.exp(own - top)
        total = jnp.sum(weight, axis=1, keepdims=True) + own_weight
        pltpu.make_async_copy(value_hbm.at[0, s], values.at[s], c_sem.at[1, s]).wait()
        mixed = []
        for g in range(KVH):
            part = slice(g * per_group, (g + 1) * per_group)
            value = values[s, :, g * HD : (g + 1) * HD]
            res = jnp.dot(weight[part].astype(BF16), value, preferred_element_type=F32)
            mixed.append(res + own_weight[part] * value_new[g : g + 1])
        attended = jnp.concatenate(mixed, axis=0) / total
        for r in range(rows):
            att[r, s] = attended[r * heads : (r + 1) * heads].astype(BF16)
        for d in range(rows):
            head_copy(s, d).start()

    for s in range(slots):
        for d in range(rows):
            head_copy(s, d).wait_send()


def layer_kernel(
    rows, cols, queries, entries, lengths, residual, gain, key_hbm, value_hbm,
    out_hbm, gate_hbm, up_hbm, down_hbm, out,
    w_out, w_gate, w_up, w_down, keys, values, qf, ef, att,
    xg, xf, xb, part, rs_in, stream, sq_out, sq_in, inv_all, xs,
    gu, core_in, sum_out, x_in, hid, acc, dn, dn_in, fin, fin_in,
    w_sem, c_sem, s1, r1, s2, r2, s3, r3, s4, r4, s5, r5, s6, r6, s7, r7,
    sa, ra, sb, rb, sc, rc_, sd, rd, s8, r8, s9, r9,
):
    side, row, col = (lax.axis_index(n) for n in ("side", "row", "col"))
    his = cols // 2
    core, hi = col % 2, col // 2
    mate = hi * 2 + (1 - core)
    half = cols // 2

    def at(s, r, c):
        return {"side": s, "row": r, "col": c}

    def rcopy(src, dst, ss, rs, dev):
        return pltpu.make_async_remote_copy(
            src_ref=src, dst_ref=dst, send_sem=ss, recv_sem=rs, device_id=dev, device_id_type=MESH
        )

    def row_peer(d):
        return lax.rem(row + d, rows)

    def col_peer(d):
        return lax.rem(col + d, cols)

    def hi_peer(d):
        return lax.rem(hi + d, his) * 2 + core

    weights = [
        pltpu.make_async_copy(h.at[0], w, w_sem.at[i])
        for i, (h, w) in enumerate(
            ((out_hbm, w_out), (gate_hbm, w_gate), (up_hbm, w_up), (down_hbm, w_down))
        )
    ]

    @pl.when(side == 1)
    def _():
        weights[0].start()

    caches = [
        pltpu.make_async_copy(h.at[0, s], v.at[s], c_sem.at[i, s])
        for s in range(keys.shape[0])
        for i, (h, v) in enumerate(((key_hbm, keys), (value_hbm, values)))
    ]

    @pl.when(side == 0)
    def _():
        for copy in caches:
            copy.start()

    barrier = pltpu.get_barrier_semaphore()

    def greet(dev):
        pl.semaphore_signal(barrier, inc=1, device_id=dev, device_id_type=MESH)

    for d in range(rows):
        greet(at(1 - side, row_peer(d), col))
    for d in range(1, cols):
        greet(at(1 - side, row, col_peer(d)))

    @pl.when(side == 1)
    def _():
        for d in range(1, rows):
            greet(at(1, row_peer(d), col))
        for d in range(1, cols):
            greet(at(1, row, col_peer(d)))
        pl.semaphore_wait(barrier, 2 * (rows + cols) - 3)

    @pl.when(side == 0)
    def _():
        pl.semaphore_wait(barrier, rows + cols - 1)

    group = residual.shape[0] // rows
    slots = group // cols
    quarter = residual.shape[0] // cols
    width = residual.shape[1]
    heads = att.shape[2]

    def head_copy(s, d):
        to = row_peer(d)
        return rcopy(
            att.at[to, s], xg.at[row, col, s], s1.at[s, d], r1.at[s, d], at(1, to, col)
        )

    @pl.when(side == 0)
    def _():
        attention(rows, queries, entries, lengths, keys, values, qf, ef, att, key_hbm, value_hbm, c_sem, head_copy)

    @pl.when(side == 1)
    def _():
        weights[0].wait()
        for copy in weights[1:]:
            copy.start()
        for s in range(slots):
            for d in range(rows):
                head_copy(s, d).wait_recv()
        mine = xg.at[:, col]
        own = rcopy(mine, mine, s2.at[0], r2.at[0], at(1, row, mate))
        own.start()
        across = [
            rcopy(mine, mine, s2.at[d], r2.at[d], at(1, row, hi_peer(d))) for d in range(1, his)
        ]
        for copy in across:
            copy.start()
        passed = []
        for d in range(1, his):
            across[d - 1].wait_recv()
            got = xg.at[:, hi_peer(his - d)]
            copy = rcopy(got, got, s2.at[his + d - 1], r2.at[his + d - 1], at(1, row, mate))
            copy.start()
            passed.append(copy)
        own.wait_recv()
        for copy in passed:
            copy.wait_recv()
        total = rows * cols * slots
        xf[...] = xg[...].astype(F32).reshape(total * heads, HD)
        for h in range(heads):
            xb[:, h * HD : (h + 1) * HD] = xf[pl.ds(h, total, stride=heads), :].astype(BF16)

        tiles, tile = part.shape[0], part.shape[3]

        def proj_copy(j, d):
            return rcopy(
                part.at[j, row_peer(d)], rs_in.at[d - 1, j], s3.at[d - 1, j], r3.at[d - 1, j],
                at(1, row_peer(d), col),
            )

        @pl.loop(0, tiles)
        def _(j):
            w = w_out[:, pl.ds(pl.multiple_of(j * tile, tile), tile)]
            res = jnp.dot(xb[...], w, preferred_element_type=F32).astype(BF16)
            part[j] = res.reshape(rows, group, tile)
            for d in range(1, rows):
                proj_copy(j, d).start()

        squares = jnp.zeros((group, 1), F32)
        my_rows = pl.ds(pl.multiple_of(row * group, group), group)
        for j in range(tiles):
            value = part[j, row].astype(F32)
            for d in range(1, rows):
                proj_copy(j, d).wait_recv()
                value = value + rs_in[d - 1, j].astype(F32)
            lanes = slice(j * tile, (j + 1) * tile)
            value = value + residual[my_rows, lanes].astype(F32)
            stream[:, lanes] = value
            squares = squares + jnp.sum(value * value, axis=1, keepdims=True)
            xs[row, :, lanes] = (value * gain[lanes].astype(F32)[None, :]).astype(BF16)
        sq_out[...] = jnp.broadcast_to(squares, sq_out.shape)

        def stream_copy(d):
            return rcopy(
                xs.at[row], xs.at[row], s4.at[d - 1], r4.at[d - 1], at(1, row_peer(d), col)
            )

        def square_copy(d):
            return rcopy(
                sq_out, sq_in.at[d - 1], s5.at[d - 1], r5.at[d - 1], at(1, row, col_peer(d))
            )

        def inv_copy(d):
            return rcopy(
                inv_all.at[row], inv_all.at[row], s6.at[d - 1], r6.at[d - 1],
                at(1, row_peer(d), col),
            )

        for d in range(1, cols):
            square_copy(d).start()
        for d in range(1, rows):
            stream_copy(d).start()
        sums = sq_out[...]
        for d in range(1, cols):
            square_copy(d).wait_recv()
            sums = sums + sq_in[d - 1]
        inv_all[row] = lax.rsqrt(sums / D + eps)
        for d in range(1, rows):
            inv_copy(d).start()
        for d in range(1, rows):
            stream_copy(d).wait_recv()
        for d in range(1, rows):
            inv_copy(d).wait_recv()
        weights[1].wait()
        weights[2].wait()
        weights[3].wait()

        steps, unit = gu.shape[0], gu.shape[5]

        def core_copy(j):
            return rcopy(gu.at[j, 1 - core], core_in.at[j], sa.at[j], ra.at[j], at(1, row, mate))

        def x_copy(j, d):
            there = lax.rem(hi + d, his)
            return rcopy(
                sum_out.at[j, there], x_in.at[d - 1, j], sb.at[d - 1, j], rb.at[d - 1, j],
                at(1, row, hi_peer(d)),
            )

        def hid_copy(j, d):
            dev = mate if d == 0 else hi_peer(d)
            return rcopy(hid.at[j, col], hid.at[j, col], sc.at[d, j], rc_.at[d, j], at(1, row, dev))

        def fwd_copy(j, d):
            got = hid.at[j, hi_peer(his - d)]
            return rcopy(got, got, sd.at[d - 1, j], rd.at[d - 1, j], at(1, row, mate))

        acc[...] = jnp.zeros_like(acc)
        lags = (0, 1, 3, 5, 6)

        @pl.loop(0, steps + lags[4])
        def _(i):
            def stage(k):
                j = i - lags[k]
                return j, jnp.logical_and(j >= 0, j < steps)

            j0, on0 = stage(0)

            @pl.when(on0)
            def _():
                at_cols = pl.ds(pl.multiple_of(j0 * unit, unit), unit)
                x = xs[...].reshape(rows * group, width)
                scale = inv_all[...].reshape(rows * group, HD)[:, :1]
                for n, w in enumerate((w_gate, w_up)):
                    res = jnp.dot(x, w[:, at_cols], preferred_element_type=F32) * scale
                    res = res.astype(BF16)
                    for q in range(cols):
                        gu[j0, q % 2, q // 2, n] = res[q * quarter : (q + 1) * quarter]
                core_copy(j0).start()

            j1, on1 = stage(1)

            @pl.when(on1)
            def _():
                core_copy(j1).wait_recv()
                sum_out[j1] = (gu[j1, core].astype(F32) + core_in[j1].astype(F32)).astype(BF16)
                for d in range(1, his):
                    x_copy(j1, d).start()

            j2, on2 = stage(2)

            @pl.when(on2)
            def _():
                both = sum_out[j2, hi].astype(F32)
                for d in range(1, his):
                    x_copy(j2, d).wait_recv()
                    both = both + x_in[d - 1, j2].astype(F32)
                gate, up = both[0], both[1]
                hid[j2, col] = (gate / (1.0 + jnp.exp(-gate)) * up).astype(BF16)
                for d in range(his):
                    hid_copy(j2, d).start()

            j3, on3 = stage(3)

            @pl.when(on3)
            def _():
                for d in range(1, his):
                    hid_copy(j3, d).wait_recv()
                    fwd_copy(j3, d).start()

            j4, on4 = stage(4)

            @pl.when(on4)
            def _():
                hid_copy(j4, 0).wait_recv()
                for d in range(1, his):
                    fwd_copy(j4, d).wait_recv()
                h = hid[j4].reshape(rows * group, unit)
                w = w_down[pl.ds(pl.multiple_of(j4 * unit, unit), unit), :]
                acc[...] += jnp.dot(h, w, preferred_element_type=F32)

        dn[...] = acc[...].astype(BF16).reshape(rows, group, width)

        def down_copy(d):
            return rcopy(
                dn.at[row_peer(d)], dn_in.at[d - 1], s7.at[d - 1], r7.at[d - 1],
                at(1, row_peer(d), col),
            )

        for d in range(1, rows):
            down_copy(d).start()
        last = stream[...] + dn[row].astype(F32)
        for d in range(1, rows):
            down_copy(d).wait_recv()
            last = last + dn_in[d - 1].astype(F32)
        last = last.astype(BF16).astype(F32)
        for c in range(cols):
            fin[c] = last[c * slots : (c + 1) * slots].astype(BF16)

        own.wait_send()
        for copy in across + passed:
            copy.wait_send()
        for d in range(1, rows):
            @pl.loop(0, tiles)
            def _(j):
                proj_copy(j, d).wait_send()
            stream_copy(d).wait_send()
            inv_copy(d).wait_send()
            down_copy(d).wait_send()
        for d in range(1, cols):
            square_copy(d).wait_send()

        @pl.loop(0, steps)
        def _(j):
            core_copy(j).wait_send()
            for d in range(his):
                hid_copy(j, d).wait_send()
            for d in range(1, his):
                x_copy(j, d).wait_send()
                fwd_copy(j, d).wait_send()

    def up_copy(d):
        return rcopy(
            fin.at[col_peer(d)], fin_in.at[col - half], s8.at[d - 1], r8.at[col - half],
            at(1, row, col_peer(d)),
        )

    def low_copy(d):
        return rcopy(
            fin.at[col_peer(d)], fin_in.at[col], s9.at[d], r8.at[col], at(0, row, col_peer(d))
        )

    @pl.when(side == 1)
    def _():
        @pl.when(col >= half)
        def _():
            for d in range(1, cols):
                up_copy(d).start()
            fin_in[col - half] = fin[col]
            for d in range(1, cols):
                up_copy(d).wait_send()

        @pl.when(col < half)
        def _():
            for d in range(cols):
                low_copy(d).start()
            for d in range(cols):
                low_copy(d).wait_send()

    for k in range(half):
        @pl.when(jnp.logical_or(side == 0, col != half + k))
        def _():
            rcopy(
                fin.at[0], fin_in.at[k], s9.at[0], r8.at[k], at(1 - side, row, col)
            ).wait_recv()
        out[:, k * width : (k + 1) * width] = fin_in[k]


def layer(rows, cols, queries, entries, lengths, residual, gain, keys, values, out_w, gate_w, up_w, down_w):
    slots = queries.shape[0]
    heads = H // rows
    total, width = residual.shape
    group, quarter, his = total // rows, total // cols, cols // 2
    ff = gate_w.shape[2]
    tile, unit = tile_of(width), tile_of(ff)
    tiles, steps = width // tile, ff // unit
    dma = pltpu.SemaphoreType.DMA
    vmem = pltpu.VMEM
    scratch = [
        vmem(out_w.shape[1:], BF16),
        vmem(gate_w.shape[1:], BF16),
        vmem(up_w.shape[1:], BF16),
        vmem(down_w.shape[1:], BF16),
        vmem(keys.shape[1:], BF16),
        vmem(values.shape[1:], BF16),
        vmem((slots, H, HD), F32),
        vmem((slots, 2 * KVH, HD), F32),
        vmem((rows, slots, heads, HD), BF16),
        vmem((rows, cols, slots, heads, HD), BF16),
        vmem((total * heads, HD), F32),
        vmem((total, heads * HD), BF16),
        vmem((tiles, rows, group, tile), BF16),
        vmem((rows - 1, tiles, group, tile), BF16),
        vmem((group, width), F32),
        vmem((group, HD), F32),
        vmem((cols - 1, group, HD), F32),
        vmem((rows, group, HD), F32),
        vmem((rows, group, width), BF16),
        vmem((steps, 2, his, 2, quarter, unit), BF16),
        vmem((steps, his, 2, quarter, unit), BF16),
        vmem((steps, his, 2, quarter, unit), BF16),
        vmem((his - 1, steps, 2, quarter, unit), BF16),
        vmem((steps, cols, quarter, unit), BF16),
        vmem((total, width), F32),
        vmem((rows, group, width), BF16),
        vmem((rows - 1, group, width), BF16),
        vmem((cols, slots, width), BF16),
        vmem((cols // 2, slots, width), BF16),
        dma((4,)), dma((2, slots)),
        dma((slots, rows)), dma((slots, rows)),
        dma((2 * his - 1,)), dma((2 * his - 1,)),
        dma((rows - 1, tiles)), dma((rows - 1, tiles)),
        dma((rows - 1,)), dma((rows - 1,)),
        dma((cols - 1,)), dma((cols - 1,)),
        dma((rows - 1,)), dma((rows - 1,)),
        dma((rows - 1,)), dma((rows - 1,)),
        dma((steps,)), dma((steps,)),
        dma((his - 1, steps)), dma((his - 1, steps)),
        dma((his, steps)), dma((his, steps)),
        dma((his - 1, steps)), dma((his - 1, steps)),
        dma((cols,)), dma((cols // 2,)),
        dma((cols,)), dma((1,)),
    ]
    in_vmem = pl.BlockSpec(memory_space=pltpu.VMEM)
    anywhere = pl.BlockSpec(memory_space=pl.ANY)

    def kernel(*refs):
        layer_kernel(rows, cols, *refs)

    weight_bytes = 2 * (out_w.size + gate_w.size + up_w.size + down_w.size)
    return pl.pallas_call(
        kernel,
        out_shape=jax.ShapeDtypeStruct((slots, width * cols // 2), BF16),
        in_specs=[in_vmem, in_vmem, pl.BlockSpec(memory_space=pltpu.SMEM), in_vmem, in_vmem]
        + [anywhere] * 6,
        out_specs=in_vmem,
        scratch_shapes=scratch,
        compiler_params=pltpu.CompilerParams(
            collective_id=0, has_side_effects=True, vmem_limit_bytes=63 * 1024 * 1024
        ),
        cost_estimate=pl.CostEstimate(
            flops=total * weight_bytes, bytes_accessed=weight_bytes, transcendentals=0
        ),
        name="layer",
    )(queries, entries, lengths, residual, gain, keys, values, out_w, gate_w, up_w, down_w)


def local(
    queries,
    new_entries,
    cache_keys,
    cache_values,
    lengths,
    residual,
    norm_gain,
    out_weight,
    gate_weight,
    up_weight,
    down_weight,
):
    return layer(
        lax.axis_size("row"), lax.axis_size("col"), queries, new_entries, lengths, residual,
        norm_gain, cache_keys, cache_values, out_weight, gate_weight, up_weight, down_weight,
    )


def solution(mesh):
    in_specs = (
        P(("row", "col"), None),
        P(("row", "col"), None),
        P("side", ("row", "col"), None, None),
        P("side", ("row", "col"), None, None),
        P(("row", "col")),
        P(None, "col"),
        P("col"),
        P("side", "row", "col"),
        P("side", "col", "row"),
        P("side", "col", "row"),
        P("side", "row", "col"),
    )
    out_specs = P(("row", "col"), "side")
    return jax.shard_map(local, mesh=mesh, in_specs=in_specs, out_specs=out_specs, check_vma=False)
```

```python
import jax
import jax.numpy as jnp
from jax import lax
from jax.experimental import pallas as pl
from jax.experimental.pallas import tpu as pltpu
from jax.sharding import PartitionSpec as P

D = 8192
H = 64
KVH = 8
HD = 128
ORIG = 64


rope_theta = 500000.0
stretch_factor = 8.0
eps = 1e-05


MESH = pl.DeviceIdType.MESH
F32 = jnp.float32
BF16 = jnp.bfloat16


def tile_of(width):
    return next(t for t in (512, 256, 128) if width % t == 0)


def attention(
    rows, queries, entries, lengths, keys, values, qf, ef, att, key_hbm, value_hbm, c_sem, head_copy
):
    slots, span, _ = keys.shape
    per_group = H // KVH
    heads = H // rows
    for s in range(slots):
        for h in range(H):
            qf[s, h : h + 1, :] = queries[s : s + 1, h * HD : (h + 1) * HD].astype(F32)
        for h in range(2 * KVH):
            ef[s, h : h + 1, :] = entries[s : s + 1, h * HD : (h + 1) * HD].astype(F32)
    lane = lax.broadcasted_iota(jnp.int32, (1, HD), 1)
    lower = lane < HD // 2
    expo = jnp.where(lower, lane, lane - HD // 2).astype(F32) * (2.0 / HD)
    fine = 16
    step = lax.broadcasted_iota(jnp.int32, (fine, HD), 0).astype(F32)
    place = lax.broadcasted_iota(jnp.int32, (H, span), 1)
    scale = HD ** (-0.5)

    def rot(vec, cosine, sine):
        return vec * cosine + pltpu.roll(vec, HD // 2, 1) * sine

    def rounded(vec):
        return vec.astype(BF16).astype(F32)

    @pl.loop(0, slots)
    def _(s):
        length = jnp.full((1, HD), lengths[s], jnp.int32).astype(F32)
        stretch = jnp.maximum(stretch_factor * (length + 1.0) / ORIG - (stretch_factor - 1.0), 1.0)
        log_base = jnp.log(jnp.full((1, HD), rope_theta, F32)) + HD / (HD - 2.0) * jnp.log(stretch)
        freq = jnp.exp(-expo * log_base)
        cos_new = jnp.cos(length * freq)
        sin_new = jnp.sin(length * freq)
        sin_new = jnp.where(lower, -sin_new, sin_new)
        cos_b, sin_b = jnp.cos(step * freq), jnp.sin(step * freq)
        cos_a, sin_a = jnp.cos(step * (fine * freq)), jnp.sin(step * (fine * freq))
        sign = jnp.where(lower, -1.0, 1.0)
        sin_b_signed, cos_b_signed = sin_b * sign, cos_b * sign
        cos_t, sin_t = [], []
        for a in range(span // fine):
            ca, sa = cos_a[a : a + 1], sin_a[a : a + 1]
            cos_t.append(ca * cos_b - sa * sin_b)
            sin_t.append(sa * cos_b_signed + ca * sin_b_signed)
        cos_t = jnp.concatenate(cos_t, axis=0)
        sin_t = jnp.concatenate(sin_t, axis=0)

        q = rounded(rot(qf[s], cos_new, sin_new))
        new = ef[s]
        key_new = rounded(rot(new[:KVH], cos_new, sin_new))
        value_new = new[KVH:]
        pltpu.make_async_copy(key_hbm.at[0, s], keys.at[s], c_sem.at[0, s]).wait()
        scores, own = [], []
        for g in range(KVH):
            q_g = q[g * per_group : (g + 1) * per_group]
            key = keys[s, :, g * HD : (g + 1) * HD].astype(F32)
            key = rot(key, cos_t, sin_t).astype(BF16)
            scores.append(
                lax.dot_general(
                    q_g.astype(BF16), key, (((1,), (1,)), ((), ())), preferred_element_type=F32
                )
            )
            own.append(jnp.sum(q_g * key_new[g : g + 1], axis=1, keepdims=True))
        scores = jnp.concatenate(scores, axis=0) * scale
        own = jnp.concatenate(own, axis=0) * scale
        valid = place < jnp.full((H, span), lengths[s], jnp.int32)
        top = jnp.maximum(jnp.max(jnp.where(valid, scores, -1e30), axis=1, keepdims=True), own)
        weight = jnp.where(valid, jnp.exp(scores - top), 0.0)
        own_weight = jnp.exp(own - top)
        total = jnp.sum(weight, axis=1, keepdims=True) + own_weight
        pltpu.make_async_copy(value_hbm.at[0, s], values.at[s], c_sem.at[1, s]).wait()
        mixed = []
        for g in range(KVH):
            part = slice(g * per_group, (g + 1) * per_group)
            value = values[s, :, g * HD : (g + 1) * HD]
            res = jnp.dot(weight[part].astype(BF16), value, preferred_element_type=F32)
            mixed.append(res + own_weight[part] * value_new[g : g + 1])
        attended = jnp.concatenate(mixed, axis=0) / total
        for r in range(rows):
            att[r, s] = attended[r * heads : (r + 1) * heads].astype(BF16)
        for d in range(rows):
            head_copy(s, d).start()

    for s in range(slots):
        for d in range(rows):
            head_copy(s, d).wait_send()


def layer_kernel(
    rows, cols, queries, entries, lengths, residual, gain, key_hbm, value_hbm,
    out_hbm, gate_hbm, up_hbm, down_hbm, out,
    w_out, w_gate, w_up, w_down, keys, values, qf, ef, att,
    xg, xf, xb, part, rs_in, stream, sq_out, sq_in, inv_all, xs,
    ahead, gu, core_in, sum_out, x_in, hid, acc, dn, dn_in, fin, fin_in,
    w_sem, c_sem, s1, r1, s2, r2, s3, r3, s4, r4, s5, r5, s6, r6, s7, r7,
    sa, ra, sb, rb, sc, rc_, sd, rd, s8, r8, s9, r9,
):
    side, row, col = (lax.axis_index(n) for n in ("side", "row", "col"))
    his = cols // 2
    core, hi = col % 2, col // 2
    mate = hi * 2 + (1 - core)
    half = cols // 2

    def at(s, r, c):
        return {"side": s, "row": r, "col": c}

    def rcopy(src, dst, ss, rs, dev):
        return pltpu.make_async_remote_copy(
            src_ref=src, dst_ref=dst, send_sem=ss, recv_sem=rs, device_id=dev, device_id_type=MESH
        )

    def row_peer(d):
        return lax.rem(row + d, rows)

    def col_peer(d):
        return lax.rem(col + d, cols)

    def hi_peer(d):
        return lax.rem(hi + d, his) * 2 + core

    weights = [
        pltpu.make_async_copy(h.at[0], w, w_sem.at[i])
        for i, (h, w) in enumerate(
            ((out_hbm, w_out), (gate_hbm, w_gate), (up_hbm, w_up), (down_hbm, w_down))
        )
    ]

    @pl.when(side == 1)
    def _():
        weights[0].start()

    caches = [
        pltpu.make_async_copy(h.at[0, s], v.at[s], c_sem.at[i, s])
        for s in range(keys.shape[0])
        for i, (h, v) in enumerate(((key_hbm, keys), (value_hbm, values)))
    ]

    @pl.when(side == 0)
    def _():
        for copy in caches:
            copy.start()

    barrier = pltpu.get_barrier_semaphore()

    def greet(dev):
        pl.semaphore_signal(barrier, inc=1, device_id=dev, device_id_type=MESH)

    for d in range(rows):
        greet(at(1 - side, row_peer(d), col))
    for d in range(1, cols):
        greet(at(1 - side, row, col_peer(d)))

    @pl.when(side == 1)
    def _():
        for d in range(1, rows):
            greet(at(1, row_peer(d), col))
        for d in range(1, cols):
            greet(at(1, row, col_peer(d)))
        pl.semaphore_wait(barrier, 2 * (rows + cols) - 3)

    @pl.when(side == 0)
    def _():
        pl.semaphore_wait(barrier, rows + cols - 1)

    group = residual.shape[0] // rows
    slots = group // cols
    quarter = residual.shape[0] // cols
    width = residual.shape[1]
    heads = att.shape[2]

    def head_copy(s, d):
        to = row_peer(d)
        return rcopy(
            att.at[to, s], xg.at[row, col, s], s1.at[s, d], r1.at[s, d], at(1, to, col)
        )

    @pl.when(side == 0)
    def _():
        attention(rows, queries, entries, lengths, keys, values, qf, ef, att, key_hbm, value_hbm, c_sem, head_copy)

    @pl.when(side == 1)
    def _():
        weights[0].wait()
        for copy in weights[1:]:
            copy.start()
        def own_copy(s):
            mine = xg.at[:, col, s]
            return rcopy(mine, mine, s2.at[0, s], r2.at[0, s], at(1, row, mate))

        def across_copy(s, d):
            mine = xg.at[:, col, s]
            return rcopy(mine, mine, s2.at[d, s], r2.at[d, s], at(1, row, hi_peer(d)))

        def passed_copy(s, d):
            got = xg.at[:, hi_peer(his - d), s]
            k = his + d - 1
            return rcopy(got, got, s2.at[k, s], r2.at[k, s], at(1, row, mate))

        for s in range(slots + 1):
            if s < slots:
                for d in range(rows):
                    head_copy(s, d).wait_recv()
                for d in range(1, his):
                    across_copy(s, d).start()
                own_copy(s).start()
            if s > 0:
                for d in range(1, his):
                    across_copy(s - 1, d).wait_recv()
                    passed_copy(s - 1, d).start()
        for s in range(slots):
            own_copy(s).wait_recv()
            for d in range(1, his):
                passed_copy(s, d).wait_recv()
        total = rows * cols * slots
        xf[...] = xg[...].astype(F32).reshape(total * heads, HD)
        for h in range(heads):
            xb[:, h * HD : (h + 1) * HD] = xf[pl.ds(h, total, stride=heads), :].astype(BF16)

        tiles, tile = part.shape[0], part.shape[3]

        def proj_copy(j, d):
            return rcopy(
                part.at[j, row_peer(d)], rs_in.at[d - 1, j], s3.at[d - 1, j], r3.at[d - 1, j],
                at(1, row_peer(d), col),
            )

        @pl.loop(0, tiles)
        def _(j):
            w = w_out[:, pl.ds(pl.multiple_of(j * tile, tile), tile)]
            res = jnp.dot(xb[...], w, preferred_element_type=F32).astype(BF16)
            part[j] = res.reshape(rows, group, tile)
            for d in range(1, rows):
                proj_copy(j, d).start()

        def stream_copy(j, d):
            chunk = xs.at[row, :, pl.ds(pl.multiple_of(j * tile, tile), tile)]
            return rcopy(
                chunk, chunk, s4.at[d - 1, j], r4.at[d - 1, j], at(1, row_peer(d), col)
            )

        squares = jnp.zeros((group, 1), F32)
        my_rows = pl.ds(pl.multiple_of(row * group, group), group)
        for j in range(tiles):
            value = part[j, row].astype(F32)
            for d in range(1, rows):
                proj_copy(j, d).wait_recv()
                value = value + rs_in[d - 1, j].astype(F32)
            lanes = slice(j * tile, (j + 1) * tile)
            value = value + residual[my_rows, lanes].astype(F32)
            stream[:, lanes] = value
            xs[row, :, lanes] = (value * gain[lanes].astype(F32)[None, :]).astype(BF16)
            for d in range(1, rows):
                stream_copy(j, d).start()
            squares = squares + jnp.sum(value * value, axis=1, keepdims=True)
        sq_out[...] = jnp.broadcast_to(squares, sq_out.shape)

        def square_copy(d):
            return rcopy(
                sq_out, sq_in.at[d - 1], s5.at[d - 1], r5.at[d - 1], at(1, row, col_peer(d))
            )

        def inv_copy(d):
            return rcopy(
                inv_all.at[row], inv_all.at[row], s6.at[d - 1], r6.at[d - 1],
                at(1, row_peer(d), col),
            )

        for d in range(1, cols):
            square_copy(d).start()
        steps, unit = gu.shape[0], gu.shape[5]
        weights[1].wait()
        weights[2].wait()

        early = tiles // 2
        for k in range(early):
            for d in range(1, rows):
                stream_copy(k, d).wait_recv()
            lanes = slice(k * tile, (k + 1) * tile)
            x_part = xs[:, :, lanes].reshape(rows * group, tile)

            @pl.loop(0, steps)
            def _(j):
                at_cols = pl.ds(pl.multiple_of(j * unit, unit), unit)
                for n, w in enumerate((w_gate, w_up)):
                    res = jnp.dot(x_part, w[lanes, at_cols], preferred_element_type=F32)
                    ahead[j, n] = res if k == 0 else ahead[j, n] + res

            if k == 0:
                sums = sq_out[...]
                for d in range(1, cols):
                    square_copy(d).wait_recv()
                    sums = sums + sq_in[d - 1]
                inv_all[row] = lax.rsqrt(sums / D + eps)
                for d in range(1, rows):
                    inv_copy(d).start()
        for k in range(early, tiles):
            for d in range(1, rows):
                stream_copy(k, d).wait_recv()
        for d in range(1, rows):
            inv_copy(d).wait_recv()
        weights[3].wait()

        def core_copy(j):
            return rcopy(gu.at[j, 1 - core], core_in.at[j], sa.at[j], ra.at[j], at(1, row, mate))

        def x_copy(j, d):
            there = lax.rem(hi + d, his)
            return rcopy(
                sum_out.at[j, there], x_in.at[d - 1, j], sb.at[d - 1, j], rb.at[d - 1, j],
                at(1, row, hi_peer(d)),
            )

        def hid_copy(j, d):
            dev = mate if d == 0 else hi_peer(d)
            return rcopy(hid.at[j, col], hid.at[j, col], sc.at[d, j], rc_.at[d, j], at(1, row, dev))

        def fwd_copy(j, d):
            got = hid.at[j, hi_peer(his - d)]
            return rcopy(got, got, sd.at[d - 1, j], rd.at[d - 1, j], at(1, row, mate))

        acc[...] = jnp.zeros_like(acc)
        lags = (0, 1, 3, 5, 6)

        @pl.loop(0, steps + lags[4])
        def _(i):
            def stage(k):
                j = i - lags[k]
                return j, jnp.logical_and(j >= 0, j < steps)

            j0, on0 = stage(0)

            @pl.when(on0)
            def _():
                at_cols = pl.ds(pl.multiple_of(j0 * unit, unit), unit)
                rest = slice(early * tile, width)
                x = xs[:, :, rest].reshape(rows * group, width - early * tile)
                scale = inv_all[...].reshape(rows * group, HD)[:, :1]
                for n, w in enumerate((w_gate, w_up)):
                    res = jnp.dot(x, w[rest, at_cols], preferred_element_type=F32)
                    res = ((res + ahead[j0, n]) * scale).astype(BF16)
                    for q in range(cols):
                        gu[j0, q % 2, q // 2, n] = res[q * quarter : (q + 1) * quarter]
                core_copy(j0).start()

            j1, on1 = stage(1)

            @pl.when(on1)
            def _():
                core_copy(j1).wait_recv()
                sum_out[j1] = (gu[j1, core].astype(F32) + core_in[j1].astype(F32)).astype(BF16)
                for d in range(1, his):
                    x_copy(j1, d).start()

            j2, on2 = stage(2)

            @pl.when(on2)
            def _():
                both = sum_out[j2, hi].astype(F32)
                for d in range(1, his):
                    x_copy(j2, d).wait_recv()
                    both = both + x_in[d - 1, j2].astype(F32)
                gate, up = both[0], both[1]
                hid[j2, col] = (gate / (1.0 + jnp.exp(-gate)) * up).astype(BF16)
                for d in range(his):
                    hid_copy(j2, d).start()

            j3, on3 = stage(3)

            @pl.when(on3)
            def _():
                for d in range(1, his):
                    hid_copy(j3, d).wait_recv()
                    fwd_copy(j3, d).start()

            j4, on4 = stage(4)

            @pl.when(on4)
            def _():
                hid_copy(j4, 0).wait_recv()
                for d in range(1, his):
                    fwd_copy(j4, d).wait_recv()

            @pl.when(jnp.logical_and(on4, j4 < steps - 1))
            def _():
                h = hid[j4].reshape(rows * group, unit)
                w = w_down[pl.ds(pl.multiple_of(j4 * unit, unit), unit), :]
                acc[...] += jnp.dot(h, w, preferred_element_type=F32)

        def down_copy(j, d):
            return rcopy(
                dn.at[j, row_peer(d)], dn_in.at[d - 1, j], s7.at[d - 1, j], r7.at[d - 1, j],
                at(1, row_peer(d), col),
            )

        h_last = hid[steps - 1].reshape(rows * group, unit)

        @pl.loop(0, tiles)
        def _(j):
            lanes = pl.ds(pl.multiple_of(j * tile, tile), tile)
            w = w_down[(steps - 1) * unit : steps * unit, lanes]
            res = acc[:, lanes] + jnp.dot(h_last, w, preferred_element_type=F32)
            dn[j] = res.astype(BF16).reshape(rows, group, tile)
            for d in range(1, rows):
                down_copy(j, d).start()

        for j in range(tiles):
            lanes = slice(j * tile, (j + 1) * tile)
            last = stream[:, lanes] + dn[j, row].astype(F32)
            for d in range(1, rows):
                down_copy(j, d).wait_recv()
                last = last + dn_in[d - 1, j].astype(F32)
            for c in range(cols):
                fin[c, :, lanes] = last[c * slots : (c + 1) * slots].astype(BF16)

        for s in range(slots):
            own_copy(s).wait_send()
            for d in range(1, his):
                across_copy(s, d).wait_send()
                passed_copy(s, d).wait_send()
        for d in range(1, rows):
            @pl.loop(0, tiles)
            def _(j):
                proj_copy(j, d).wait_send()
                stream_copy(j, d).wait_send()
                down_copy(j, d).wait_send()
            inv_copy(d).wait_send()
        for d in range(1, cols):
            square_copy(d).wait_send()

        @pl.loop(0, steps)
        def _(j):
            core_copy(j).wait_send()
            for d in range(his):
                hid_copy(j, d).wait_send()
            for d in range(1, his):
                x_copy(j, d).wait_send()
                fwd_copy(j, d).wait_send()

    def up_copy(d):
        return rcopy(
            fin.at[col_peer(d)], fin_in.at[col - half], s8.at[d - 1], r8.at[col - half],
            at(1, row, col_peer(d)),
        )

    def low_copy(d):
        return rcopy(
            fin.at[col_peer(d)], fin_in.at[col], s9.at[d], r8.at[col], at(0, row, col_peer(d))
        )

    @pl.when(side == 1)
    def _():
        @pl.when(col >= half)
        def _():
            for d in range(1, cols):
                up_copy(d).start()
            fin_in[col - half] = fin[col]
            for d in range(1, cols):
                up_copy(d).wait_send()

        @pl.when(col < half)
        def _():
            for d in range(cols):
                low_copy(d).start()
            for d in range(cols):
                low_copy(d).wait_send()

    for k in range(half):
        @pl.when(jnp.logical_or(side == 0, col != half + k))
        def _():
            rcopy(
                fin.at[0], fin_in.at[k], s9.at[0], r8.at[k], at(1 - side, row, col)
            ).wait_recv()
        out[:, k * width : (k + 1) * width] = fin_in[k].astype(F32)


def layer(rows, cols, queries, entries, lengths, residual, gain, keys, values, out_w, gate_w, up_w, down_w):
    slots = queries.shape[0]
    heads = H // rows
    total, width = residual.shape
    group, quarter, his = total // rows, total // cols, cols // 2
    ff = gate_w.shape[2]
    tile, unit = width // 4, tile_of(ff)
    tiles, steps = width // tile, ff // unit
    dma = pltpu.SemaphoreType.DMA
    vmem = pltpu.VMEM
    scratch = [
        vmem(out_w.shape[1:], BF16),
        vmem(gate_w.shape[1:], BF16),
        vmem(up_w.shape[1:], BF16),
        vmem(down_w.shape[1:], BF16),
        vmem(keys.shape[1:], BF16),
        vmem(values.shape[1:], BF16),
        vmem((slots, H, HD), F32),
        vmem((slots, 2 * KVH, HD), F32),
        vmem((rows, slots, heads, HD), BF16),
        vmem((rows, cols, slots, heads, HD), BF16),
        vmem((total * heads, HD), F32),
        vmem((total, heads * HD), BF16),
        vmem((tiles, rows, group, tile), BF16),
        vmem((rows - 1, tiles, group, tile), BF16),
        vmem((group, width), F32),
        vmem((group, HD), F32),
        vmem((cols - 1, group, HD), F32),
        vmem((rows, group, HD), F32),
        vmem((rows, group, width), BF16),
        vmem((steps, 2, total, unit), F32),
        vmem((steps, 2, his, 2, quarter, unit), BF16),
        vmem((steps, his, 2, quarter, unit), BF16),
        vmem((steps, his, 2, quarter, unit), BF16),
        vmem((his - 1, steps, 2, quarter, unit), BF16),
        vmem((steps, cols, quarter, unit), BF16),
        vmem((total, width), F32),
        vmem((tiles, rows, group, tile), BF16),
        vmem((rows - 1, tiles, group, tile), BF16),
        vmem((cols, slots, width), BF16),
        vmem((cols // 2, slots, width), BF16),
        dma((4,)), dma((2, slots)),
        dma((slots, rows)), dma((slots, rows)),
        dma((2 * his - 1, slots)), dma((2 * his - 1, slots)),
        dma((rows - 1, tiles)), dma((rows - 1, tiles)),
        dma((rows - 1, tiles)), dma((rows - 1, tiles)),
        dma((cols - 1,)), dma((cols - 1,)),
        dma((rows - 1,)), dma((rows - 1,)),
        dma((rows - 1, tiles)), dma((rows - 1, tiles)),
        dma((steps,)), dma((steps,)),
        dma((his - 1, steps)), dma((his - 1, steps)),
        dma((his, steps)), dma((his, steps)),
        dma((his - 1, steps)), dma((his - 1, steps)),
        dma((cols,)), dma((cols // 2,)),
        dma((cols,)), dma((1,)),
    ]
    in_vmem = pl.BlockSpec(memory_space=pltpu.VMEM)
    anywhere = pl.BlockSpec(memory_space=pl.ANY)

    def kernel(*refs):
        layer_kernel(rows, cols, *refs)

    weight_bytes = 2 * (out_w.size + gate_w.size + up_w.size + down_w.size)
    return pl.pallas_call(
        kernel,
        out_shape=jax.ShapeDtypeStruct((slots, width * cols // 2), F32),
        in_specs=[in_vmem, in_vmem, pl.BlockSpec(memory_space=pltpu.SMEM), in_vmem, in_vmem]
        + [anywhere] * 6,
        out_specs=in_vmem,
        scratch_shapes=scratch,
        compiler_params=pltpu.CompilerParams(
            collective_id=0, has_side_effects=True, vmem_limit_bytes=63 * 1024 * 1024
        ),
        cost_estimate=pl.CostEstimate(
            flops=total * weight_bytes, bytes_accessed=weight_bytes, transcendentals=0
        ),
        name="layer",
    )(queries, entries, lengths, residual, gain, keys, values, out_w, gate_w, up_w, down_w).astype(BF16)


def local(
    queries,
    new_entries,
    cache_keys,
    cache_values,
    lengths,
    residual,
    norm_gain,
    out_weight,
    gate_weight,
    up_weight,
    down_weight,
):
    return layer(
        lax.axis_size("row"), lax.axis_size("col"), queries, new_entries, lengths, residual,
        norm_gain, cache_keys, cache_values, out_weight, gate_weight, up_weight, down_weight,
    )


def solution(mesh):
    in_specs = (
        P(("row", "col"), None),
        P(("row", "col"), None),
        P("side", ("row", "col"), None, None),
        P("side", ("row", "col"), None, None),
        P(("row", "col")),
        P(None, "col"),
        P("col"),
        P("side", "row", "col"),
        P("side", "col", "row"),
        P("side", "col", "row"),
        P("side", "row", "col"),
    )
    out_specs = P(("row", "col"), "side")
    return jax.shard_map(local, mesh=mesh, in_specs=in_specs, out_specs=out_specs, check_vma=False)
```

```python
import jax
import jax.numpy as jnp
from jax import lax
from jax.experimental import pallas as pl
from jax.experimental.pallas import tpu as pltpu
from jax.sharding import PartitionSpec as P

D = 8192
H = 64
KVH = 8
HD = 128
ORIG = 64


rope_theta = 500000.0
stretch_factor = 8.0
eps = 1e-05


MESH = pl.DeviceIdType.MESH
F32 = jnp.float32
BF16 = jnp.bfloat16


def tile_of(width):
    return next(t for t in (512, 256, 128) if width % t == 0)


def attention(
    rows, queries, entries, lengths, keys, values, qf, ef, att, key_hbm, value_hbm, c_sem, head_copy
):
    slots, span, _ = keys.shape
    per_group = H // KVH
    heads = H // rows
    for s in range(slots):
        for h in range(H):
            qf[s, h : h + 1, :] = queries[s : s + 1, h * HD : (h + 1) * HD].astype(F32)
        for h in range(2 * KVH):
            ef[s, h : h + 1, :] = entries[s : s + 1, h * HD : (h + 1) * HD].astype(F32)
    lane = lax.broadcasted_iota(jnp.int32, (1, HD), 1)
    lower = lane < HD // 2
    expo = jnp.where(lower, lane, lane - HD // 2).astype(F32) * (2.0 / HD)
    fine = 16
    step = lax.broadcasted_iota(jnp.int32, (fine, HD), 0).astype(F32)
    place = lax.broadcasted_iota(jnp.int32, (H, span), 1)
    scale = HD ** (-0.5)

    def rot(vec, cosine, sine):
        return vec * cosine + pltpu.roll(vec, HD // 2, 1) * sine

    def rounded(vec):
        return vec.astype(BF16).astype(F32)

    @pl.loop(0, slots)
    def _(s):
        length = jnp.full((1, HD), lengths[s], jnp.int32).astype(F32)
        stretch = jnp.maximum(stretch_factor * (length + 1.0) / ORIG - (stretch_factor - 1.0), 1.0)
        log_base = jnp.log(jnp.full((1, HD), rope_theta, F32)) + HD / (HD - 2.0) * jnp.log(stretch)
        freq = jnp.exp(-expo * log_base)
        cos_new = jnp.cos(length * freq)
        sin_new = jnp.sin(length * freq)
        sin_new = jnp.where(lower, -sin_new, sin_new)
        cos_b, sin_b = jnp.cos(step * freq), jnp.sin(step * freq)
        cos_a, sin_a = jnp.cos(step * (fine * freq)), jnp.sin(step * (fine * freq))
        sign = jnp.where(lower, -1.0, 1.0)
        sin_b_signed, cos_b_signed = sin_b * sign, cos_b * sign
        cos_t, sin_t = [], []
        for a in range(span // fine):
            ca, sa = cos_a[a : a + 1], sin_a[a : a + 1]
            cos_t.append(ca * cos_b - sa * sin_b)
            sin_t.append(sa * cos_b_signed + ca * sin_b_signed)
        cos_t = jnp.concatenate(cos_t, axis=0)
        sin_t = jnp.concatenate(sin_t, axis=0)

        q = rounded(rot(qf[s], cos_new, sin_new))
        new = ef[s]
        key_new = rounded(rot(new[:KVH], cos_new, sin_new))
        value_new = new[KVH:]
        pltpu.make_async_copy(key_hbm.at[0, s], keys.at[s], c_sem.at[0, s]).wait()
        scores, own = [], []
        for g in range(KVH):
            q_g = q[g * per_group : (g + 1) * per_group]
            key = keys[s, :, g * HD : (g + 1) * HD].astype(F32)
            key = rot(key, cos_t, sin_t).astype(BF16)
            scores.append(
                lax.dot_general(
                    q_g.astype(BF16), key, (((1,), (1,)), ((), ())), preferred_element_type=F32
                )
            )
            own.append(jnp.sum(q_g * key_new[g : g + 1], axis=1, keepdims=True))
        scores = jnp.concatenate(scores, axis=0) * scale
        own = jnp.concatenate(own, axis=0) * scale
        valid = place < jnp.full((H, span), lengths[s], jnp.int32)
        top = jnp.maximum(jnp.max(jnp.where(valid, scores, -1e30), axis=1, keepdims=True), own)
        weight = jnp.where(valid, jnp.exp(scores - top), 0.0)
        own_weight = jnp.exp(own - top)
        total = jnp.sum(weight, axis=1, keepdims=True) + own_weight
        pltpu.make_async_copy(value_hbm.at[0, s], values.at[s], c_sem.at[1, s]).wait()
        mixed = []
        for g in range(KVH):
            part = slice(g * per_group, (g + 1) * per_group)
            value = values[s, :, g * HD : (g + 1) * HD]
            res = jnp.dot(weight[part].astype(BF16), value, preferred_element_type=F32)
            mixed.append(res + own_weight[part] * value_new[g : g + 1])
        attended = jnp.concatenate(mixed, axis=0) / total
        for r in range(rows):
            att[r, s] = attended[r * heads : (r + 1) * heads].astype(BF16)
        for d in range(rows):
            head_copy(s, d).start()

    for s in range(slots):
        for d in range(rows):
            head_copy(s, d).wait_send()


def layer_kernel(
    rows, cols, queries, entries, lengths, residual, gain, key_hbm, value_hbm,
    out_hbm, gate_hbm, up_hbm, down_hbm, out,
    w_out, w_gate, w_up, w_down, keys, values, qf, ef, att,
    xg, xf, xb, part, rs_in, stream, sq_out, sq_in, inv_all, xs,
    ahead, gu, core_in, sum_out, x_in, hid, acc, dn, dn_in, fin, fin_in,
    w_sem, c_sem, s1, r1, s2, r2, s3, r3, s4, r4, s5, r5, s6, r6, s7, r7,
    sa, ra, sb, rb, sc, rc_, sd, rd, s8, r8, s9, r9,
):
    side, row, col = (lax.axis_index(n) for n in ("side", "row", "col"))
    his = cols // 2
    core, hi = col % 2, col // 2
    mate = hi * 2 + (1 - core)
    half = cols // 2

    def at(s, r, c):
        return {"side": s, "row": r, "col": c}

    def rcopy(src, dst, ss, rs, dev):
        return pltpu.make_async_remote_copy(
            src_ref=src, dst_ref=dst, send_sem=ss, recv_sem=rs, device_id=dev, device_id_type=MESH
        )

    def row_peer(d):
        return lax.rem(row + d, rows)

    def col_peer(d):
        return lax.rem(col + d, cols)

    def hi_peer(d):
        return lax.rem(hi + d, his) * 2 + core

    tiles, steps = part.shape[0], gu.shape[0]

    def blocks_of(k, count):
        hbm, ref = ((out_hbm, w_out), (gate_hbm, w_gate), (up_hbm, w_up), (down_hbm, w_down))[k]
        size = ref.shape[0] // count

        def block(j):
            lines = pl.ds(pl.multiple_of(j * size, size), size)
            return pltpu.make_async_copy(hbm.at[0, lines], ref.at[lines], w_sem.at[k, j])

        return block

    out_block, down_block = blocks_of(0, tiles), blocks_of(3, steps)
    gate_block, up_block = blocks_of(1, tiles), blocks_of(2, tiles)

    @pl.when(side == 1)
    def _():
        for k in range(tiles):
            out_block(k).start()

    caches = [
        pltpu.make_async_copy(h.at[0, s], v.at[s], c_sem.at[i, s])
        for s in range(keys.shape[0])
        for i, (h, v) in enumerate(((key_hbm, keys), (value_hbm, values)))
    ]

    @pl.when(side == 0)
    def _():
        for copy in caches:
            copy.start()

    barrier = pltpu.get_barrier_semaphore()

    def greet(dev):
        pl.semaphore_signal(barrier, inc=1, device_id=dev, device_id_type=MESH)

    for d in range(rows):
        greet(at(1 - side, row_peer(d), col))
    for d in range(1, cols):
        greet(at(1 - side, row, col_peer(d)))

    @pl.when(side == 1)
    def _():
        for d in range(1, rows):
            greet(at(1, row_peer(d), col))
        for d in range(1, cols):
            greet(at(1, row, col_peer(d)))
        pl.semaphore_wait(barrier, 2 * (rows + cols) - 3)

    @pl.when(side == 0)
    def _():
        pl.semaphore_wait(barrier, rows + cols - 1)

    group = residual.shape[0] // rows
    slots = group // cols
    quarter = residual.shape[0] // cols
    width = residual.shape[1]
    heads = att.shape[2]

    def head_copy(s, d):
        to = row_peer(d)
        return rcopy(
            att.at[to, s], xg.at[row, col, s], s1.at[s, d], r1.at[s, d], at(1, to, col)
        )

    @pl.when(side == 0)
    def _():
        attention(rows, queries, entries, lengths, keys, values, qf, ef, att, key_hbm, value_hbm, c_sem, head_copy)

    @pl.when(side == 1)
    def _():
        early = tiles // 2
        for k in range(tiles):
            out_block(k).wait()
        for k in range(early):
            gate_block(k).start()
            up_block(k).start()
        def own_copy(s):
            mine = xg.at[:, col, s]
            return rcopy(mine, mine, s2.at[0, s], r2.at[0, s], at(1, row, mate))

        def across_copy(s, d):
            mine = xg.at[:, col, s]
            return rcopy(mine, mine, s2.at[d, s], r2.at[d, s], at(1, row, hi_peer(d)))

        def passed_copy(s, d):
            got = xg.at[:, hi_peer(his - d), s]
            k = his + d - 1
            return rcopy(got, got, s2.at[k, s], r2.at[k, s], at(1, row, mate))

        for s in range(slots + 1):
            if s < slots:
                for d in range(rows):
                    head_copy(s, d).wait_recv()
                for d in range(1, his):
                    across_copy(s, d).start()
                own_copy(s).start()
                if s == 0:
                    for k in range(early, tiles):
                        gate_block(k).start()
                        up_block(k).start()
            if s > 0:
                for d in range(1, his):
                    across_copy(s - 1, d).wait_recv()
                    passed_copy(s - 1, d).start()
        for s in range(slots):
            own_copy(s).wait_recv()
            for d in range(1, his):
                passed_copy(s, d).wait_recv()
        for j in range(steps):
            down_block(j).start()
        total = rows * cols * slots
        xf[...] = xg[...].astype(F32).reshape(total * heads, HD)
        for h in range(heads):
            xb[:, h * HD : (h + 1) * HD] = xf[pl.ds(h, total, stride=heads), :].astype(BF16)

        tile = part.shape[3]

        def proj_copy(j, d):
            return rcopy(
                part.at[j, row_peer(d)], rs_in.at[d - 1, j], s3.at[d - 1, j], r3.at[d - 1, j],
                at(1, row_peer(d), col),
            )

        @pl.loop(0, tiles, unroll=True)
        def _(j):
            w = w_out[:, pl.ds(pl.multiple_of(j * tile, tile), tile)]
            res = jnp.dot(xb[...], w, preferred_element_type=F32).astype(BF16)
            part[j] = res.reshape(rows, group, tile)
            for d in range(1, rows):
                proj_copy(j, d).start()

        def stream_copy(j, d):
            chunk = xs.at[row, :, pl.ds(pl.multiple_of(j * tile, tile), tile)]
            return rcopy(
                chunk, chunk, s4.at[d - 1, j], r4.at[d - 1, j], at(1, row_peer(d), col)
            )

        squares = jnp.zeros((group, 1), F32)
        my_rows = pl.ds(pl.multiple_of(row * group, group), group)
        for j in range(tiles):
            value = part[j, row].astype(F32)
            for d in range(1, rows):
                proj_copy(j, d).wait_recv()
                value = value + rs_in[d - 1, j].astype(F32)
            lanes = slice(j * tile, (j + 1) * tile)
            value = value + residual[my_rows, lanes].astype(F32)
            stream[:, lanes] = value
            xs[row, :, lanes] = (value * gain[lanes].astype(F32)[None, :]).astype(BF16)
            for d in range(1, rows):
                stream_copy(j, d).start()
            squares = squares + jnp.sum(value * value, axis=1, keepdims=True)
        sq_out[...] = jnp.broadcast_to(squares, sq_out.shape)

        def square_copy(d):
            return rcopy(
                sq_out, sq_in.at[d - 1], s5.at[d - 1], r5.at[d - 1], at(1, row, col_peer(d))
            )

        def inv_copy(d):
            return rcopy(
                inv_all.at[row], inv_all.at[row], s6.at[d - 1], r6.at[d - 1],
                at(1, row_peer(d), col),
            )

        for d in range(1, cols):
            square_copy(d).start()
        unit = gu.shape[5]

        for k in range(early):
            gate_block(k).wait()
            up_block(k).wait()
            for d in range(1, rows):
                stream_copy(k, d).wait_recv()
            lanes = slice(k * tile, (k + 1) * tile)
            x_part = xs[:, :, lanes].reshape(rows * group, tile)

            @pl.loop(0, steps, unroll=True)
            def _(j):
                at_cols = pl.ds(pl.multiple_of(j * unit, unit), unit)
                for n, w in enumerate((w_gate, w_up)):
                    res = jnp.dot(x_part, w[lanes, at_cols], preferred_element_type=F32)
                    ahead[j, n] = res if k == 0 else ahead[j, n] + res

            if k == 0:
                sums = sq_out[...]
                for d in range(1, cols):
                    square_copy(d).wait_recv()
                    sums = sums + sq_in[d - 1]
                inv_all[row] = lax.rsqrt(sums / D + eps)
                for d in range(1, rows):
                    inv_copy(d).start()
        for k in range(early, tiles):
            gate_block(k).wait()
            up_block(k).wait()
            for d in range(1, rows):
                stream_copy(k, d).wait_recv()
        for d in range(1, rows):
            inv_copy(d).wait_recv()

        def core_copy(j):
            return rcopy(gu.at[j, 1 - core], core_in.at[j], sa.at[j], ra.at[j], at(1, row, mate))

        def x_copy(j, d):
            there = lax.rem(hi + d, his)
            return rcopy(
                sum_out.at[j, there], x_in.at[d - 1, j], sb.at[d - 1, j], rb.at[d - 1, j],
                at(1, row, hi_peer(d)),
            )

        def hid_copy(j, d):
            dev = mate if d == 0 else hi_peer(d)
            return rcopy(hid.at[j, col], hid.at[j, col], sc.at[d, j], rc_.at[d, j], at(1, row, dev))

        def fwd_copy(j, d):
            got = hid.at[j, hi_peer(his - d)]
            return rcopy(got, got, sd.at[d - 1, j], rd.at[d - 1, j], at(1, row, mate))

        acc[...] = jnp.zeros_like(acc)
        lags = (0, 1, 3, 5, 6)

        @pl.loop(0, steps + lags[4])
        def _(i):
            def stage(k):
                j = i - lags[k]
                return j, jnp.logical_and(j >= 0, j < steps)

            j0, on0 = stage(0)

            @pl.when(on0)
            def _():
                at_cols = pl.ds(pl.multiple_of(j0 * unit, unit), unit)
                rest = slice(early * tile, width)
                x = xs[:, :, rest].reshape(rows * group, width - early * tile)
                scale = inv_all[...].reshape(rows * group, HD)[:, :1]
                for n, w in enumerate((w_gate, w_up)):
                    res = jnp.dot(x, w[rest, at_cols], preferred_element_type=F32)
                    res = ((res + ahead[j0, n]) * scale).astype(BF16)
                    for q in range(cols):
                        gu[j0, q % 2, q // 2, n] = res[q * quarter : (q + 1) * quarter]
                core_copy(j0).start()

            j1, on1 = stage(1)

            @pl.when(on1)
            def _():
                core_copy(j1).wait_recv()
                sum_out[j1] = (gu[j1, core].astype(F32) + core_in[j1].astype(F32)).astype(BF16)
                for d in range(1, his):
                    x_copy(j1, d).start()

            j2, on2 = stage(2)

            @pl.when(on2)
            def _():
                both = sum_out[j2, hi].astype(F32)
                for d in range(1, his):
                    x_copy(j2, d).wait_recv()
                    both = both + x_in[d - 1, j2].astype(F32)
                gate, up = both[0], both[1]
                hid[j2, col] = (gate / (1.0 + jnp.exp(-gate)) * up).astype(BF16)
                for d in range(his):
                    hid_copy(j2, d).start()

            j3, on3 = stage(3)

            @pl.when(on3)
            def _():
                for d in range(1, his):
                    hid_copy(j3, d).wait_recv()
                    fwd_copy(j3, d).start()

            j4, on4 = stage(4)

            @pl.when(on4)
            def _():
                down_block(j4).wait()
                hid_copy(j4, 0).wait_recv()
                for d in range(1, his):
                    fwd_copy(j4, d).wait_recv()

            @pl.when(jnp.logical_and(on4, j4 < steps - 1))
            def _():
                h = hid[j4].reshape(rows * group, unit)
                w = w_down[pl.ds(pl.multiple_of(j4 * unit, unit), unit), :]
                acc[...] += jnp.dot(h, w, preferred_element_type=F32)

        def down_copy(j, d):
            return rcopy(
                dn.at[j, row_peer(d)], dn_in.at[d - 1, j], s7.at[d - 1, j], r7.at[d - 1, j],
                at(1, row_peer(d), col),
            )

        h_last = hid[steps - 1].reshape(rows * group, unit)

        @pl.loop(0, tiles)
        def _(j):
            lanes = pl.ds(pl.multiple_of(j * tile, tile), tile)
            w = w_down[(steps - 1) * unit : steps * unit, lanes]
            res = acc[:, lanes] + jnp.dot(h_last, w, preferred_element_type=F32)
            dn[j] = res.astype(BF16).reshape(rows, group, tile)
            for d in range(1, rows):
                down_copy(j, d).start()

        for j in range(tiles):
            lanes = slice(j * tile, (j + 1) * tile)
            last = stream[:, lanes] + dn[j, row].astype(F32)
            for d in range(1, rows):
                down_copy(j, d).wait_recv()
                last = last + dn_in[d - 1, j].astype(F32)
            for c in range(cols):
                fin[c, :, lanes] = last[c * slots : (c + 1) * slots].astype(BF16)

        for s in range(slots):
            own_copy(s).wait_send()
            for d in range(1, his):
                across_copy(s, d).wait_send()
                passed_copy(s, d).wait_send()
        for d in range(1, rows):
            @pl.loop(0, tiles)
            def _(j):
                proj_copy(j, d).wait_send()
                stream_copy(j, d).wait_send()
                down_copy(j, d).wait_send()
            inv_copy(d).wait_send()
        for d in range(1, cols):
            square_copy(d).wait_send()

        @pl.loop(0, steps)
        def _(j):
            core_copy(j).wait_send()
            for d in range(his):
                hid_copy(j, d).wait_send()
            for d in range(1, his):
                x_copy(j, d).wait_send()
                fwd_copy(j, d).wait_send()

    def up_copy(d):
        return rcopy(
            fin.at[col_peer(d)], fin_in.at[col - half], s8.at[d - 1], r8.at[col - half],
            at(1, row, col_peer(d)),
        )

    def low_copy(d):
        return rcopy(
            fin.at[col_peer(d)], fin_in.at[col], s9.at[d], r8.at[col], at(0, row, col_peer(d))
        )

    @pl.when(side == 1)
    def _():
        @pl.when(col >= half)
        def _():
            for d in range(1, cols):
                up_copy(d).start()
            fin_in[col - half] = fin[col]
            for d in range(1, cols):
                up_copy(d).wait_send()

        @pl.when(col < half)
        def _():
            for d in range(cols):
                low_copy(d).start()
            for d in range(cols):
                low_copy(d).wait_send()

    for k in range(half):
        @pl.when(jnp.logical_or(side == 0, col != half + k))
        def _():
            rcopy(
                fin.at[0], fin_in.at[k], s9.at[0], r8.at[k], at(1 - side, row, col)
            ).wait_recv()
        out[:, k * width : (k + 1) * width] = fin_in[k].astype(F32)


def layer(rows, cols, queries, entries, lengths, residual, gain, keys, values, out_w, gate_w, up_w, down_w):
    slots = queries.shape[0]
    heads = H // rows
    total, width = residual.shape
    group, quarter, his = total // rows, total // cols, cols // 2
    ff = gate_w.shape[2]
    tile, unit = width // 4, tile_of(ff)
    tiles, steps = width // tile, ff // unit
    dma = pltpu.SemaphoreType.DMA
    vmem = pltpu.VMEM
    scratch = [
        vmem(out_w.shape[1:], BF16),
        vmem(gate_w.shape[1:], BF16),
        vmem(up_w.shape[1:], BF16),
        vmem(down_w.shape[1:], BF16),
        vmem(keys.shape[1:], BF16),
        vmem(values.shape[1:], BF16),
        vmem((slots, H, HD), F32),
        vmem((slots, 2 * KVH, HD), F32),
        vmem((rows, slots, heads, HD), BF16),
        vmem((rows, cols, slots, heads, HD), BF16),
        vmem((total * heads, HD), F32),
        vmem((total, heads * HD), BF16),
        vmem((tiles, rows, group, tile), BF16),
        vmem((rows - 1, tiles, group, tile), BF16),
        vmem((group, width), F32),
        vmem((group, HD), F32),
        vmem((cols - 1, group, HD), F32),
        vmem((rows, group, HD), F32),
        vmem((rows, group, width), BF16),
        vmem((steps, 2, total, unit), F32),
        vmem((steps, 2, his, 2, quarter, unit), BF16),
        vmem((steps, his, 2, quarter, unit), BF16),
        vmem((steps, his, 2, quarter, unit), BF16),
        vmem((his - 1, steps, 2, quarter, unit), BF16),
        vmem((steps, cols, quarter, unit), BF16),
        vmem((total, width), F32),
        vmem((tiles, rows, group, tile), BF16),
        vmem((rows - 1, tiles, group, tile), BF16),
        vmem((cols, slots, width), BF16),
        vmem((cols // 2, slots, width), BF16),
        dma((4, max(tiles, steps))), dma((2, slots)),
        dma((slots, rows)), dma((slots, rows)),
        dma((2 * his - 1, slots)), dma((2 * his - 1, slots)),
        dma((rows - 1, tiles)), dma((rows - 1, tiles)),
        dma((rows - 1, tiles)), dma((rows - 1, tiles)),
        dma((cols - 1,)), dma((cols - 1,)),
        dma((rows - 1,)), dma((rows - 1,)),
        dma((rows - 1, tiles)), dma((rows - 1, tiles)),
        dma((steps,)), dma((steps,)),
        dma((his - 1, steps)), dma((his - 1, steps)),
        dma((his, steps)), dma((his, steps)),
        dma((his - 1, steps)), dma((his - 1, steps)),
        dma((cols,)), dma((cols // 2,)),
        dma((cols,)), dma((1,)),
    ]
    in_vmem = pl.BlockSpec(memory_space=pltpu.VMEM)
    anywhere = pl.BlockSpec(memory_space=pl.ANY)

    def kernel(*refs):
        layer_kernel(rows, cols, *refs)

    weight_bytes = 2 * (out_w.size + gate_w.size + up_w.size + down_w.size)
    return pl.pallas_call(
        kernel,
        out_shape=jax.ShapeDtypeStruct((slots, width * cols // 2), F32),
        in_specs=[in_vmem, in_vmem, pl.BlockSpec(memory_space=pltpu.SMEM), in_vmem, in_vmem]
        + [anywhere] * 6,
        out_specs=in_vmem,
        scratch_shapes=scratch,
        compiler_params=pltpu.CompilerParams(
            collective_id=0, has_side_effects=True, vmem_limit_bytes=63 * 1024 * 1024
        ),
        cost_estimate=pl.CostEstimate(
            flops=total * weight_bytes, bytes_accessed=weight_bytes, transcendentals=0
        ),
        name="layer",
    )(queries, entries, lengths, residual, gain, keys, values, out_w, gate_w, up_w, down_w).astype(BF16)


def local(
    queries,
    new_entries,
    cache_keys,
    cache_values,
    lengths,
    residual,
    norm_gain,
    out_weight,
    gate_weight,
    up_weight,
    down_weight,
):
    return layer(
        lax.axis_size("row"), lax.axis_size("col"), queries, new_entries, lengths, residual,
        norm_gain, cache_keys, cache_values, out_weight, gate_weight, up_weight, down_weight,
    )


def solution(mesh):
    in_specs = (
        P(("row", "col"), None),
        P(("row", "col"), None),
        P("side", ("row", "col"), None, None),
        P("side", ("row", "col"), None, None),
        P(("row", "col")),
        P(None, "col"),
        P("col"),
        P("side", "row", "col"),
        P("side", "col", "row"),
        P("side", "col", "row"),
        P("side", "row", "col"),
    )
    out_specs = P(("row", "col"), "side")
    return jax.shard_map(local, mesh=mesh, in_specs=in_specs, out_specs=out_specs, check_vma=False)
```
